128 devices in a mesh: outer: 16 (over x_lo, z, core), inner: 8 (over y, x_hi).
Axes of the slice: x: 4 (x_hi: 2, x_lo: 2; x = x_hi * 2 + x_lo), y: 4, z: 4, core: 2. Of those that a mesh axis runs over, the one named last changes fastest.
Arguments:
- raw_q: bfloat16 [128, 512, 2048], P(('outer', 'inner')), may hold values from -170 to 170
- raw_k: bfloat16 [128, 512, 2048], P(('outer', 'inner')), may hold values from -7 to 7
- raw_v: bfloat16 [128, 512, 2048], P(('outer', 'inner')), may hold values from -6 to 6
- raw_grad: bfloat16 [128, 512, 2048], P(('outer', 'inner')), may hold values from -6 to 6
- beacon_q: bfloat16 [128, 4, 2048], P(('outer', 'inner')), may hold values from -6 to 6
- beacon_k: bfloat16 [128, 4, 2048], P(('outer', 'inner')), may hold values from -6 to 6
- beacon_v: bfloat16 [128, 4, 2048], P(('outer', 'inner')), may hold values from -6 to 6
- beacon_grad: bfloat16 [128, 4, 2048], P(('outer', 'inner')), may hold values from -6 to 6
- assign: int32 [128], replicated, may hold values from 0 to 127, each once
- prefix: int32 [128], replicated, may hold values from 0 to 127, as said below
Outputs:
- raw_dq: bfloat16 [128, 512, 2048], P(('outer', 'inner'))
- raw_dk: bfloat16 [128, 512, 2048], P(('outer', 'inner'))
- raw_dv: bfloat16 [128, 512, 2048], P(('outer', 'inner'))
- beacon_dq: bfloat16 [128, 4, 2048], P(('outer', 'inner'))
- beacon_dk: bfloat16 [128, 4, 2048], P(('outer', 'inner'))
- beacon_dv: bfloat16 [128, 4, 2048], P(('outer', 'inner'))
The draws below stay inside these ranges and needn't reach their ends.
Inputs may be any that keep to these rules, and one draw needn't show every extreme that they name: `assign`: each stretch number appears once. prefix[c] is at most c; the last stretch sees all earlier stretches.
All inputs are finite; a program needn't handle non-finite values.
Results may differ from the reference program's by a relative error of at most 0.015.
Values may be sent and summed in bfloat16 or wider, within the bound.
No kernel may reach another device: no remote copies, remote signals or barrier semaphores. Data moves between devices by JAX's collectives and lax.ppermute only.
A program may use at most 128 MiB of HBM per device.

```python
import jax
import jax.numpy as jnp
from jax import lax

HEADS = 16
HEAD_DIM = 128
STRETCH = 512
BEACONS = 4
FEAT = 2048
NCHUNK = 128


def drawn_pair(key):
    base_key = jnp.clip(jax.random.normal(jax.random.fold_in(key, 11), (NCHUNK, STRETCH, FEAT), jnp.float32), -6.0, 6.0)
    base_query = jax.random.normal(jax.random.fold_in(key, 12), (NCHUNK, STRETCH, FEAT), jnp.float32)
    return (base_key, base_query)


def draw_raw_k(key, part):
    base_key, base_query = drawn_pair(key)
    return base_key.astype(jnp.bfloat16)


def draw_raw_q(key, part):
    base_key, base_query = drawn_pair(key)
    return base_query.astype(jnp.bfloat16)


def draw_prefix(key, part):
    key = jax.random.fold_in(key, 5)
    stretches = jnp.arange(NCHUNK, dtype=jnp.int32)
    picked = jax.random.randint(key, (NCHUNK,), 0, stretches + 1, dtype=jnp.int32)
    return jnp.where(stretches == NCHUNK - 1, stretches, picked)


def level_of(stream_key, dims, shards, low, largest):
    loudness = 1.0
    for dim, parts in shards:
        heights = jax.random.uniform(jax.random.fold_in(jax.random.fold_in(stream_key, 6), dim), (parts,), jnp.float32, low / len(shards), largest / len(shards))
        loudness = loudness * jnp.repeat(jnp.exp(heights), dims[dim] // parts).reshape((-1,) + (1,) * (len(dims) - 1 - dim))
    return loudness


def noise(key, shape, spread, reach, shards=(), kind=jnp.bfloat16):
    entries = spread * jax.random.normal(key, shape, jnp.float32)
    if shards:
        entries = entries * level_of(key, shape, shards, -0.22, 0.18)
    return jnp.clip(entries, -reach, reach).astype(kind)


def setup_inputs(seed: int = 0) -> dict:
    seeds = jax.random.split(jax.random.key(seed), 11)
    return {
        "raw_q": draw_raw_q(jax.random.fold_in(seeds[10], 71), 0),
        "raw_k": draw_raw_k(jax.random.fold_in(seeds[10], 71), 0),
        "raw_v": noise(seeds[2], (NCHUNK, STRETCH, FEAT), 1.0, 6.0, ((0, 128),)),
        "raw_grad": noise(seeds[3], (NCHUNK, STRETCH, FEAT), 1.0, 6.0, ((0, 128),)),
        "beacon_q": noise(seeds[4], (NCHUNK, BEACONS, FEAT), 1.0, 6.0, ((0, 128),)),
        "beacon_k": noise(seeds[5], (NCHUNK, BEACONS, FEAT), 1.0, 6.0, ((0, 128),)),
        "beacon_v": noise(seeds[6], (NCHUNK, BEACONS, FEAT), 1.0, 6.0, ((0, 128),)),
        "beacon_grad": noise(seeds[7], (NCHUNK, BEACONS, FEAT), 1.0, 6.0, ((0, 128),)),
        "assign": jax.random.permutation(seeds[8], NCHUNK).astype(jnp.int32),
        "prefix": draw_prefix(jax.random.fold_in(seeds[10], 71), 0),
    }


def visibility(total_rows, stretch_rows, key_stretch, stretch, lowest):
    rows = jnp.arange(total_rows, dtype=jnp.int32)[:, None]
    far_seen = (key_stretch >= lowest) & (key_stretch < stretch)
    far_block = jnp.broadcast_to(far_seen[None, :], (total_rows, key_stretch.shape[0]))
    columns = jnp.arange(stretch_rows, dtype=jnp.int32)[None, :]
    near_block = (columns <= rows) | (rows >= stretch_rows)
    own_columns = jnp.arange(total_rows - stretch_rows, dtype=jnp.int32)[None, :]
    own_block = (rows >= stretch_rows) & (own_columns <= rows - stretch_rows)
    return jnp.concatenate([far_block, near_block, own_block], axis=1)


def head_step(queries, keys, values, grads, visible, head):
    width = HEAD_DIM
    score_scale = width ** -0.5
    head_query = lax.dynamic_slice_in_dim(queries, head * width, width, 1)
    head_key = lax.dynamic_slice_in_dim(keys, head * width, width, 1)
    head_value = lax.dynamic_slice_in_dim(values, head * width, width, 1)
    head_grad = lax.dynamic_slice_in_dim(grads, head * width, width, 1)
    scores = jnp.dot(head_query, head_key.T, preferred_element_type=jnp.float32) * score_scale
    scores = jnp.where(visible, scores, -1e30)
    row_top = jnp.max(scores, axis=1, keepdims=True)
    weights = jnp.exp(scores - row_top)
    probs = weights / jnp.sum(weights, axis=1, keepdims=True)
    probs_low = probs.astype(jnp.bfloat16)
    dprobs = jnp.dot(head_grad, head_value.T, preferred_element_type=jnp.float32)
    row_inner = jnp.sum(probs * dprobs, axis=1, keepdims=True)
    dscores = (probs * (dprobs - row_inner) * score_scale).astype(jnp.bfloat16)
    dvalue = jnp.dot(probs_low.T, head_grad, preferred_element_type=jnp.float32)
    dquery = jnp.dot(dscores, head_key, preferred_element_type=jnp.float32)
    dkey = jnp.dot(dscores.T, head_query, preferred_element_type=jnp.float32)
    return dquery, dkey, dvalue


def merge_heads(stacked):
    return jnp.transpose(stacked, (1, 0, 2)).reshape(stacked.shape[1], stacked.shape[0] * stacked.shape[2])


def slot_grads(queries, keys, values, grads, visible):
    def one_head(head):
        return head_step(queries, keys, values, grads, visible, head)
    dquery, dkey, dvalue = lax.map(one_head, jnp.arange(HEADS, dtype=jnp.int32))
    return merge_heads(dquery), merge_heads(dkey), merge_heads(dvalue)


def reference(raw_q, raw_k, raw_v, raw_grad, beacon_q, beacon_k, beacon_v, beacon_grad, assign, prefix):
    slots = raw_q.shape[0]
    stretch_rows = raw_q.shape[1]
    features = raw_q.shape[2]
    far_rows = slots * BEACONS
    far_keys = beacon_k.reshape(far_rows, features)
    far_values = beacon_v.reshape(far_rows, features)
    key_stretch = assign[jnp.arange(far_rows, dtype=jnp.int32) // BEACONS]

    def step(carry, slot):
        acc_key, acc_value = carry
        stretch = assign[slot]
        lowest = stretch - prefix[stretch]
        queries = jnp.concatenate([raw_q[slot], beacon_q[slot]], axis=0)
        keys = jnp.concatenate([far_keys, raw_k[slot], beacon_k[slot]], axis=0)
        values = jnp.concatenate([far_values, raw_v[slot], beacon_v[slot]], axis=0)
        grads = jnp.concatenate([raw_grad[slot], beacon_grad[slot]], axis=0)
        visible = visibility(stretch_rows + BEACONS, stretch_rows, key_stretch, stretch, lowest)
        dquery, dkey, dvalue = slot_grads(queries, keys, values, grads, visible)
        acc_key = acc_key + dkey[:far_rows]
        acc_value = acc_value + dvalue[:far_rows]
        outs = (dquery[:stretch_rows].astype(jnp.bfloat16), dquery[stretch_rows:].astype(jnp.bfloat16),
                dkey[far_rows:far_rows + stretch_rows].astype(jnp.bfloat16),
                dvalue[far_rows:far_rows + stretch_rows].astype(jnp.bfloat16),
                dkey[far_rows + stretch_rows:], dvalue[far_rows + stretch_rows:])
        return (acc_key, acc_value), outs

    start = (jnp.zeros((far_rows, features), jnp.float32), jnp.zeros((far_rows, features), jnp.float32))
    (acc_key, acc_value), outs = lax.scan(step, start, jnp.arange(slots, dtype=jnp.int32))
    raw_dq, beacon_dq, raw_dk, raw_dv, own_key, own_value = outs
    beacon_dk = (own_key + acc_key.reshape(slots, BEACONS, features)).astype(jnp.bfloat16)
    beacon_dv = (own_value + acc_value.reshape(slots, BEACONS, features)).astype(jnp.bfloat16)
    return (raw_dq, raw_dk, raw_dv, beacon_dq, beacon_dk, beacon_dv)
```

```python
import math

import jax
import jax.numpy as jnp
import numpy as np
from jax import lax
from jax.experimental import pallas as pl
from jax.experimental.pallas import tpu as pltpu
from jax.sharding import Mesh
from jax.sharding import PartitionSpec as P

HEAD_DIM = 128
PAIR = 2 * HEAD_DIM
BEACONS = 4
STRETCH = 512
FEAT = 2048
PAIRS = FEAT // PAIR
LANES = 128
HALF = 256
BLOCK = 64
SCALE = HEAD_DIM ** (-0.5)
LOG_SCALE = SCALE * math.log2(math.e)
HIDDEN = -1e30
F32 = jnp.float32
BF16 = jnp.bfloat16

NAMES = ("x_lo", "z", "core", "y", "x_hi")
SIZES = (2, 4, 2, 4, 2)

X0, X1, Y0, Y1, Z0, Z1 = 1, 2, 4, 8, 16, 32
STEPS = ((Z0, Z1, Y0, Y1, X0, X1), (X0, X1, Z0, Z1, Y0, Y1))


def gray(position):
    return position ^ (position >> 1)


def slot_of(label, core):
    x, y, z = (gray((label >> shift) & 3) for shift in (0, 2, 4))
    return ((((x & 1) * 4 + z) * 2 + core) * 4 + y) * 2 + (x >> 1)


def exchange(value, step):
    pairs = []
    for label in range(64):
        for core in range(2):
            partner = label ^ STEPS[core][step]
            pairs.append((slot_of(label, core), slot_of(partner, core)))
    return lax.ppermute(value, NAMES, sorted(pairs))


def swap(value):
    return lax.ppermute(value, "core", [(0, 1), (1, 0)])


def gather(beacon_k, beacon_v):
    both = jnp.concatenate([beacon_k, beacon_v], axis=1)
    for step in range(4):
        both = jnp.concatenate([both, exchange(both, step)], axis=0)
    key, value = both[:, :FEAT], both[:, FEAT:]
    for first, second in ((4, 5), (5, 4)):
        got_key, got_value = exchange(key, first), exchange(value, second)
        key = jnp.concatenate([key, got_key], axis=0)
        value = jnp.concatenate([value, got_value], axis=0)
    return key, value, swap(key), swap(value)


def added(kept, got):
    return (kept.astype(F32) + got.astype(F32)).astype(BF16)


def scatter(key, value, key_other, value_other):
    got_key, got_value = swap(key_other), swap(value_other)
    key, value = added(key, got_key), added(value, got_value)
    for first, second in ((5, 4), (4, 5)):
        half = key.shape[0] // 2
        got_key, got_value = exchange(key[half:], first), exchange(value[half:], second)
        key, value = added(key[:half], got_key), added(value[:half], got_value)
    both = jnp.concatenate([key, value], axis=1)
    for step in (3, 2, 1):
        half = both.shape[0] // 2
        both = added(both[:half], exchange(both[half:], step))
    half = both.shape[0] // 2
    both = both[:half].astype(F32) + exchange(both[half:], 0).astype(F32)
    return both[:, :FEAT], both[:, FEAT:]


def far_bias(assign, prefix):
    coords = [lax.axis_index(name) for name in NAMES]
    x_lo, z, core, y, x_hi = coords
    mine = gray(x_hi * 2 + x_lo) | (gray(y) << 2) | (gray(z) << 4)
    tables = np.zeros((2, BLOCK * BEACONS), np.int32)
    for which in range(2):
        for row in range(BLOCK * BEACONS):
            place = row // BEACONS
            tables[which, row] = sum(
                bit for step, bit in enumerate(STEPS[which]) if place >> step & 1
            )
    first = jnp.where(core == 0, tables[0], tables[1])
    second = jnp.where(core == 0, tables[1], tables[0])
    slots = jnp.concatenate([slot_of(mine ^ first, core), slot_of(mine ^ second, 1 - core)])
    numbers = jnp.arange(assign.shape[0], dtype=jnp.int32)
    own = slot_of(mine, core)
    stretch = jnp.sum(jnp.where(numbers == own, assign, 0))
    lowest = stretch - jnp.sum(jnp.where(numbers == stretch, prefix, 0))
    seen = (assign >= lowest) & (assign < stretch)
    hit = (slots[:, None] == numbers[None, :]) & seen[None, :]
    visible = jnp.any(hit, axis=1, keepdims=True)
    return jnp.broadcast_to(jnp.where(visible, 0.0, HIDDEN).astype(F32), (2 * HALF, LANES))


def spread(rows):
    pairs = rows.reshape(BEACONS, PAIRS, 2, HEAD_DIM).transpose(1, 2, 0, 3)
    zero = jnp.zeros((PAIRS, BEACONS, HEAD_DIM), rows.dtype)
    top = jnp.concatenate([pairs[:, 0], zero], axis=2)
    low = jnp.concatenate([zero, pairs[:, 1]], axis=2)
    rest = jnp.zeros((PAIRS, LANES - 2 * BEACONS, PAIR), rows.dtype)
    return jnp.concatenate([top, low, rest], axis=1)


def nt(a, b):
    return lax.dot_general(a, b, (((1,), (1,)), ((), ())), preferred_element_type=F32)


def nn(a, b):
    return lax.dot_general(a, b, (((1,), (0,)), ((), ())), preferred_element_type=F32)


def tn(a, b):
    return lax.dot_general(a, b, (((0,), (0,)), ((), ())), preferred_element_type=F32)


def top_of(scores):
    return jnp.max(scores, axis=0, keepdims=True)


def sum_of(values):
    return jnp.sum(values, axis=0, keepdims=True)


def causal(scores):
    rows = lax.broadcasted_iota(jnp.int32, scores.shape, 0)
    columns = lax.broadcasted_iota(jnp.int32, scores.shape, 1)
    return jnp.where(rows <= columns, scores, HIDDEN)


def own_mask(scores):
    rows = lax.broadcasted_iota(jnp.int32, scores.shape, 0)
    columns = lax.broadcasted_iota(jnp.int32, scores.shape, 1)
    return jnp.where((rows <= (columns & 3)) & (rows < BEACONS), scores, HIDDEN)


def power(scores, top):
    return jnp.exp2((scores - top) * LOG_SCALE)


def stats_of(parts):
    top = top_of(parts[0][0])
    for scores, _ in parts[1:]:
        top = jnp.maximum(top, top_of(scores))
    total = inner = None
    for scores, dprobs in parts:
        weights = power(scores, top)
        part, part_inner = sum_of(weights), sum_of(weights * dprobs)
        total = part if total is None else total + part
        inner = part_inner if inner is None else inner + part_inner
    return top, total, inner


def head(index):
    return slice(index * HEAD_DIM, (index + 1) * HEAD_DIM)


def raw_parts(q, k, v, g):
    low, high = slice(0, HALF), slice(HALF, 2 * HALF)
    s00 = causal(nt(k[low], q[low]))
    s01 = nt(k[low], q[high])
    s11 = causal(nt(k[high], q[high]))
    d00 = nt(v[low], g[low])
    d01 = nt(v[low], g[high])
    d11 = nt(v[high], g[high])
    return (s00, d00), (s01, d01), (s11, d11)


def stats_kernel(q_ref, k_ref, v_ref, g_ref, bk_ref, bv_ref, qb_ref, gb_ref, st_ref):
    for index in range(2):
        columns = head(index)
        p00, p01, p11 = raw_parts(
            q_ref[:, columns], k_ref[:, columns], v_ref[:, columns], g_ref[:, columns]
        )
        for place, stats in ((0, stats_of([p00])), (HALF, stats_of([p01, p11]))):
            for row, entry in enumerate(stats):
                st_ref[3 * index + row : 3 * index + row + 1, place : place + HALF] = entry
    qb, gb = qb_ref[...], gb_ref[...]
    far = nt(k_ref[...], qb), nt(v_ref[...], gb)
    own = own_mask(nt(bk_ref[...], qb)), nt(bv_ref[...], gb)
    for row, entry in enumerate(stats_of([far, own])):
        st_ref[row : row + 1, STRETCH:] = entry


def merged(scores, dprobs, stats):
    top, total, inner = stats
    new_top = jnp.maximum(top, top_of(scores))
    weights = power(scores, new_top)
    factor = power(top, new_top)
    total = total * factor + sum_of(weights)
    inner = inner * factor + sum_of(weights * dprobs)
    scaled = 1.0 / total
    return weights, (new_top, scaled, inner * scaled)


def split_grad(weights, dprobs, stats):
    _, scaled, inner = stats
    probs = weights * scaled
    return probs.astype(BF16), (probs * (dprobs - inner)).astype(BF16)


def aligned(value):
    return jnp.concatenate(
        [value[block * BLOCK : (block + 1) * BLOCK] for block in (0, 2, 1, 3)], axis=0
    )


def far_kernel(
    q_ref, g_ref, fk_ref, fv_ref, ok_ref, ov_ref, qb_ref, gb_ref, bias_ref, st_ref,
    dk_ref, dv_ref, dok_ref, dov_ref, dq_ref, dqb_ref, out_ref,
):
    bias = bias_ref[...]
    wide = jnp.concatenate([bias] * 4, axis=1)
    key = jnp.concatenate([fk_ref[...], ok_ref[...]], axis=0)
    value = jnp.concatenate([aligned(fv_ref[...]), aligned(ov_ref[...])], axis=0)
    qb, gb = qb_ref[...], gb_ref[...]
    scores = nt(key, qb) + bias
    dprobs = nt(value, gb)
    stats = tuple(st_ref[row : row + 1, STRETCH:] for row in range(3))
    weights, stats = merged(scores, dprobs, stats)
    for row, entry in enumerate(stats):
        out_ref[row : row + 1, STRETCH:] = entry
    probs, dscores = split_grad(weights, dprobs, stats)
    dkey, dvalue = nn(dscores, qb), nn(probs, gb)
    dqb_ref[...] = tn(dscores, key)[: 2 * BEACONS]
    for index in range(2):
        columns = head(index)
        q, g = q_ref[:, columns], g_ref[:, columns]
        scores = nt(key[:, columns], q) + wide
        dprobs = nt(value[:, columns], g)
        stats = tuple(st_ref[3 * index + row : 3 * index + row + 1, :STRETCH] for row in range(3))
        weights, stats = merged(scores, dprobs, stats)
        for row, entry in enumerate(stats):
            out_ref[3 * index + row : 3 * index + row + 1, :STRETCH] = entry
        probs, dscores = split_grad(weights, dprobs, stats)
        head_key = ((nn(dscores, q) + dkey[:, columns]) * SCALE).astype(BF16)
        head_value = (nn(probs, g) + dvalue[:, columns]).astype(BF16)
        dk_ref[:, columns] = head_key[:HALF]
        dok_ref[:, columns] = head_key[HALF:]
        dv_ref[:, columns] = aligned(head_value[:HALF])
        dov_ref[:, columns] = aligned(head_value[HALF:])
        dq_ref[columns, :] = tn(key[:, columns], dscores)


def grads(scores, dprobs, stats):
    return split_grad(power(scores, stats[0]), dprobs, stats)


def raw_kernel(
    q_ref, k_ref, v_ref, g_ref, bk_ref, bv_ref, qb_ref, gb_ref, st_ref, dqf_ref, dqb_ref,
    dq_ref, dk_ref, dv_ref, dbq_ref, own_k_ref, own_v_ref,
):
    qb, gb = qb_ref[...], gb_ref[...]
    key, value = k_ref[...], v_ref[...]
    stats = tuple(st_ref[row : row + 1, STRETCH:] for row in range(3))
    probs, dscores = grads(nt(key, qb), nt(value, gb), stats)
    dkey, dvalue = nn(dscores, qb), nn(probs, gb)
    dqb = tn(dscores, key)[: 2 * BEACONS] + dqb_ref[...]
    own_key = bk_ref[...]
    probs, dscores = grads(own_mask(nt(own_key, qb)), nt(bv_ref[...], gb), stats)
    own_k_ref[...] = nn(dscores, qb)[: 2 * BEACONS] * SCALE
    own_v_ref[...] = nn(probs, gb)[: 2 * BEACONS]
    dqb = (dqb + tn(dscores, own_key)[: 2 * BEACONS]) * SCALE
    dbq_ref[:, head(0)] = dqb[:BEACONS, head(0)].astype(BF16)
    dbq_ref[:, head(1)] = dqb[BEACONS:, head(1)].astype(BF16)
    low, high = slice(0, HALF), slice(HALF, 2 * HALF)
    for index in range(2):
        columns = head(index)
        q, k, v, g = q_ref[:, columns], key[:, columns], value[:, columns], g_ref[:, columns]
        stats = tuple(st_ref[3 * index + row : 3 * index + row + 1, :STRETCH] for row in range(3))
        first = tuple(entry[:, low] for entry in stats)
        second = tuple(entry[:, high] for entry in stats)
        p00, p01, p11 = raw_parts(q, k, v, g)
        probs00, ds00 = grads(*p00, first)
        probs01, ds01 = grads(*p01, second)
        probs11, ds11 = grads(*p11, second)
        dk_ref[low, columns] = (
            (nn(ds00, q[low]) + nn(ds01, q[high]) + dkey[low, columns]) * SCALE
        ).astype(BF16)
        dk_ref[high, columns] = ((nn(ds11, q[high]) + dkey[high, columns]) * SCALE).astype(BF16)
        dv_ref[low, columns] = (
            nn(probs00, g[low]) + nn(probs01, g[high]) + dvalue[low, columns]
        ).astype(BF16)
        dv_ref[high, columns] = (nn(probs11, g[high]) + dvalue[high, columns]).astype(BF16)
        dq_low = dqf_ref[columns, low] + tn(k[low], ds00)
        dq_high = dqf_ref[columns, high] + tn(k[low], ds01) + tn(k[high], ds11)
        dq_ref[low, columns] = (dq_low.T * SCALE).astype(BF16)
        dq_ref[high, columns] = (dq_high.T * SCALE).astype(BF16)


def three(rows):
    return pl.BlockSpec((None, rows, PAIR), lambda pair: (0, 0, pair))


def two(rows):
    return pl.BlockSpec((rows, PAIR), lambda pair: (0, pair))


def paired(rows, columns):
    return pl.BlockSpec((None, rows, columns), lambda pair: (pair, 0, 0))


def shape(dims, dtype):
    return jax.ShapeDtypeStruct(dims, dtype)


def params():
    return pltpu.CompilerParams(
        dimension_semantics=("arbitrary",), vmem_limit_bytes=40 * 1024 * 1024
    )


def cost(flops, moved):
    return pl.CostEstimate(flops=flops, bytes_accessed=moved, transcendentals=0)


STAT_LANES = STRETCH + LANES


def on_device(
    raw_q, raw_k, raw_v, raw_grad, beacon_q, beacon_k, beacon_v, beacon_grad, assign, prefix
):
    far_key, far_value, other_key, other_value = gather(beacon_k[0], beacon_v[0])
    bias = far_bias(assign, prefix)
    qb, gb = spread(beacon_q[0]), spread(beacon_grad[0])
    fill = jnp.zeros((12, FEAT), BF16)
    own_k = jnp.concatenate([beacon_k[0], fill], axis=0)
    own_v = jnp.concatenate([beacon_v[0], fill], axis=0)
    stat = shape((PAIRS, 8, STAT_LANES), F32)
    raw = three(STRETCH)
    spreads = [paired(LANES, PAIR)] * 2
    stats = pl.pallas_call(
        stats_kernel,
        grid=(PAIRS,),
        in_specs=[raw] * 4 + [two(16)] * 2 + spreads,
        out_specs=paired(8, STAT_LANES),
        out_shape=stat,
        compiler_params=params(),
        cost_estimate=cost(4 * 10**9, 8 * 2**20),
        name="raw_stats",
    )(raw_q, raw_k, raw_v, raw_grad, own_k, own_v, qb, gb)
    half = shape((HALF, FEAT), BF16)
    dk, dv, dok, dov, dqf, dqb, stats = pl.pallas_call(
        far_kernel,
        grid=(PAIRS,),
        in_specs=[raw] * 2
        + [two(HALF)] * 4
        + spreads
        + [pl.BlockSpec((2 * HALF, LANES), lambda pair: (0, 0)), paired(8, STAT_LANES)],
        out_specs=[two(HALF)] * 4
        + [
            pl.BlockSpec((PAIR, STRETCH), lambda pair: (pair, 0)),
            paired(8, PAIR),
            paired(8, STAT_LANES),
        ],
        out_shape=[half] * 4 + [shape((FEAT, STRETCH), F32), shape((PAIRS, 8, PAIR), F32), stat],
        compiler_params=params(),
        cost_estimate=cost(6 * 10**9, 16 * 2**20),
        name="far_grads",
    )(raw_q, raw_grad, far_key, far_value, other_key, other_value, qb, gb, bias, stats)
    summed_key, summed_value = scatter(dk, dv, dok, dov)
    raw_out = shape((1, STRETCH, FEAT), BF16)
    raw_dq, raw_dk, raw_dv, beacon_dq, own_dk, own_dv = pl.pallas_call(
        raw_kernel,
        grid=(PAIRS,),
        in_specs=[raw] * 4
        + [two(16)] * 2
        + spreads
        + [
            paired(8, STAT_LANES),
            pl.BlockSpec((PAIR, STRETCH), lambda pair: (pair, 0)),
            paired(8, PAIR),
        ],
        out_specs=[raw] * 3 + [three(BEACONS)] + [two(8)] * 2,
        out_shape=[raw_out] * 3
        + [shape((1, BEACONS, FEAT), BF16)]
        + [shape((8, FEAT), F32)] * 2,
        compiler_params=params(),
        cost_estimate=cost(6 * 10**9, 20 * 2**20),
        name="raw_grads",
    )(raw_q, raw_k, raw_v, raw_grad, own_k, own_v, qb, gb, stats, dqf, dqb)
    beacon_dk = (own_dk[:BEACONS] + summed_key).astype(BF16)[None]
    beacon_dv = (own_dv[:BEACONS] + summed_value).astype(BF16)[None]
    return (raw_dq, raw_dk, raw_dv, beacon_dq, beacon_dk, beacon_dv)


def solution(mesh):
    named = Mesh(mesh.devices.reshape(SIZES), NAMES)
    placed = P(NAMES, None, None)
    return jax.shard_map(
        on_device,
        mesh=named,
        in_specs=(placed,) * 8 + (P(), P()),
        out_specs=(placed,) * 6,
        check_vma=False,
    )
```

```python
import math

import jax
import jax.numpy as jnp
import numpy as np
from jax import lax
from jax.experimental import pallas as pl
from jax.experimental.pallas import tpu as pltpu
from jax.sharding import Mesh
from jax.sharding import PartitionSpec as P

HEAD_DIM = 128
PAIR = 2 * HEAD_DIM
BEACONS = 4
STRETCH = 512
FEAT = 2048
PAIRS = FEAT // PAIR
LANES = 128
HALF = 256
BLOCK = 64
SCALE = HEAD_DIM ** (-0.5)
LOG_SCALE = SCALE * math.log2(math.e)
HIDDEN = -1e30
F32 = jnp.float32
BF16 = jnp.bfloat16

NAMES = ("x_lo", "z", "core", "y", "x_hi")
SIZES = (2, 4, 2, 4, 2)

X0, X1, Y0, Y1, Z0, Z1 = 1, 2, 4, 8, 16, 32
STEPS = ((Z0, Z1, Y0, Y1, X0, X1), (X0, X1, Z0, Z1, Y0, Y1))


def gray(position):
    return position ^ (position >> 1)


def slot_of(label, core):
    x, y, z = (gray((label >> shift) & 3) for shift in (0, 2, 4))
    return ((((x & 1) * 4 + z) * 2 + core) * 4 + y) * 2 + (x >> 1)


def exchange(value, step):
    pairs = []
    for label in range(64):
        for core in range(2):
            partner = label ^ STEPS[core][step]
            pairs.append((slot_of(label, core), slot_of(partner, core)))
    return lax.ppermute(value, NAMES, sorted(pairs))


def swap(value):
    return lax.ppermute(value, "core", [(0, 1), (1, 0)])


def beside(values, token, work):
    values, token = lax.optimization_barrier((values, token))
    return lax.optimization_barrier(work(values, token))


def joined(kept, got, axis=0):
    return lax.optimization_barrier(jnp.concatenate([kept, got], axis=axis))


def added(first, *more):
    total = first.astype(F32)
    for term in more:
        total = total + term.astype(F32)
    return total.astype(BF16)


def mask_kernel(place_ref, assign_ref, prefix_ref, bias_ref):
    mine, core, own = place_ref[0, 0], place_ref[0, 1], place_ref[0, 2]
    numbers = lax.broadcasted_iota(jnp.int32, (1, LANES), 1)
    assign, prefix = assign_ref[...], prefix_ref[...]

    def pick(values, index):
        return jnp.sum(jnp.where(numbers == index, values, 0).astype(F32), axis=1, keepdims=True)

    stretch = pick(assign, own).astype(jnp.int32)
    lowest = stretch - pick(prefix, stretch).astype(jnp.int32)
    seen = jnp.where((assign >= lowest) & (assign < stretch), 1.0, 0.0)
    place = lax.broadcasted_iota(jnp.int32, (HALF, LANES), 0) >> 2
    labels = []
    for steps in STEPS:
        label = jnp.full((HALF, LANES), mine, jnp.int32)
        for step, bit in enumerate(steps):
            label = label ^ (((place >> step) & 1) * bit)
        labels.append(label)
    for half in range(2):
        label = jnp.where(core == half, labels[0], labels[1])
        slots = slot_of(label, core if half == 0 else 1 - core)
        found = jnp.sum(jnp.where(slots == numbers, seen, 0.0), axis=1, keepdims=True)
        rows = slice(half * HALF, (half + 1) * HALF)
        bias_ref[rows] = jnp.broadcast_to(jnp.where(found > 0.5, 0.0, HIDDEN), (HALF, LANES))


def far_bias(assign, prefix):
    x_lo, z, core, y, x_hi = (lax.axis_index(name) for name in NAMES)
    mine = gray(x_hi * 2 + x_lo) | (gray(y) << 2) | (gray(z) << 4)
    place = jnp.stack([mine, core, slot_of(mine, core)]).astype(jnp.int32).reshape(1, 3)
    line = pl.BlockSpec((1, LANES), lambda: (0, 0))
    return pl.pallas_call(
        mask_kernel,
        in_specs=[pl.BlockSpec(memory_space=pltpu.SMEM), line, line],
        out_specs=pl.BlockSpec((2 * HALF, LANES), lambda: (0, 0)),
        out_shape=jax.ShapeDtypeStruct((2 * HALF, LANES), F32),
        name="far_mask",
    )(place, assign.reshape(1, LANES), prefix.reshape(1, LANES))


def spread(rows):
    twice = jnp.concatenate([rows.astype(F32)] * 2, axis=0)
    row = lax.broadcasted_iota(jnp.int32, twice.shape, 0)
    column = lax.broadcasted_iota(jnp.int32, twice.shape, 1)
    kept = jnp.where((row < BEACONS) == (column < HEAD_DIM), twice, 0.0)
    rest = jnp.zeros((LANES - 2 * BEACONS, rows.shape[1]), F32)
    return jnp.concatenate([kept, rest], axis=0).astype(BF16)


def padded(rows):
    rest = jnp.zeros((12, rows.shape[1]), F32)
    return jnp.concatenate([rows.astype(F32), rest], axis=0).astype(BF16)


def nt(a, b):
    return lax.dot_general(a, b, (((1,), (1,)), ((), ())), preferred_element_type=F32)


def nn(a, b):
    return lax.dot_general(a, b, (((1,), (0,)), ((), ())), preferred_element_type=F32)


def tn(a, b):
    return lax.dot_general(a, b, (((0,), (0,)), ((), ())), preferred_element_type=F32)


def top_of(scores):
    return jnp.max(scores, axis=0, keepdims=True)


def sum_of(values):
    return jnp.sum(values, axis=0, keepdims=True)


def causal(scores):
    rows = lax.broadcasted_iota(jnp.int32, scores.shape, 0)
    columns = lax.broadcasted_iota(jnp.int32, scores.shape, 1)
    return jnp.where(rows <= columns, scores, HIDDEN)


def own_mask(scores):
    rows = lax.broadcasted_iota(jnp.int32, scores.shape, 0)
    columns = lax.broadcasted_iota(jnp.int32, scores.shape, 1)
    return jnp.where((rows <= (columns & 3)) & (rows < BEACONS), scores, HIDDEN)


def power(scores, top):
    return jnp.exp2((scores - top) * LOG_SCALE)


def stats_of(parts):
    top = top_of(parts[0][0])
    for scores, _ in parts[1:]:
        top = jnp.maximum(top, top_of(scores))
    total = inner = None
    for scores, dprobs in parts:
        weights = power(scores, top)
        part, part_inner = sum_of(weights), sum_of(weights * dprobs)
        total = part if total is None else total + part
        inner = part_inner if inner is None else inner + part_inner
    return top, total, inner


def head(index):
    return slice(index * HEAD_DIM, (index + 1) * HEAD_DIM)


def raw_parts(q, k, v, g):
    low, high = slice(0, HALF), slice(HALF, 2 * HALF)
    s00 = causal(nt(k[low], q[low]))
    s01 = nt(k[low], q[high])
    s11 = causal(nt(k[high], q[high]))
    d00 = nt(v[low], g[low])
    d01 = nt(v[low], g[high])
    d11 = nt(v[high], g[high])
    return (s00, d00), (s01, d01), (s11, d11)


def stats_kernel(q_ref, k_ref, v_ref, g_ref, bq_ref, bk_ref, bv_ref, bg_ref, *refs):
    st_ref = refs[-1]
    qb, gb = spread(bq_ref[...]), spread(bg_ref[...])

    def products(index):
        if index < 0:
            raw = nt(k_ref[...], qb), nt(v_ref[...], gb)
            return raw, (own_mask(nt(padded(bk_ref[...]), qb)), nt(padded(bv_ref[...]), gb))
        columns = head(index)
        return raw_parts(
            q_ref[:, columns], k_ref[:, columns], v_ref[:, columns], g_ref[:, columns]
        )

    def store(index, *parts):
        if index < 0:
            found = ((STRETCH, LANES, stats_of(parts)),)
        else:
            p00, p01, p11 = parts
            found = ((0, HALF, stats_of([p00])), (HALF, HALF, stats_of([p01, p11])))
        for place, width, stats in found:
            for row, entry in enumerate(stats):
                row += 3 * max(index, 0)
                st_ref[row : row + 1, place : place + width] = entry

    pipelined([(-1,), (0,), (1,)], products, store)


def units_of(q_ref):
    return [(pair, index) for pair in range(q_ref.shape[1] // PAIR) for index in (-1, 0, 1)]


def columns_of(pair, index):
    if index < 0:
        return slice(pair * PAIR, (pair + 1) * PAIR)
    return head(2 * pair + index)


def block_columns(pair, index, value):
    start = 2 * pair * PAIR + (PAIR if value else 0)
    if index < 0:
        return slice(start, start + PAIR)
    return slice(start + index * HEAD_DIM, start + (index + 1) * HEAD_DIM)


def lanes_of(index):
    return slice(STRETCH, STAT_LANES) if index < 0 else slice(0, STRETCH)


def read_stats(ref, pair, index):
    base = 3 * max(index, 0)
    return tuple(ref[pair, base + row : base + row + 1, lanes_of(index)] for row in range(3))


def write_stats(ref, pair, index, stats):
    base = 3 * max(index, 0)
    for row, entry in enumerate(stats):
        ref[pair, base + row : base + row + 1, lanes_of(index)] = entry


def final_of(stats):
    top, total, inner = stats
    scaled = 1.0 / total
    return top, scaled, inner * scaled


def spread_pairs(*refs):
    pairs = refs[0].shape[1] // PAIR
    return [
        [spread(ref[:, pair * PAIR : (pair + 1) * PAIR]) for ref in refs] for pair in range(pairs)
    ]


def rows_of(refs, columns):
    return jnp.concatenate([ref[:, columns] for ref in refs], axis=0)


def pipelined(units, first, second):
    ready = first(*units[0])
    for place, unit in enumerate(units):
        now = ready
        if place + 1 < len(units):
            ready = first(*units[place + 1])
        second(*unit, *now)


def weighed(scores, dprobs, before, pair, index):
    known = [read_stats(ref, pair, index) for ref in before]
    top = top_of(scores)
    for stats in known:
        top = jnp.maximum(top, stats[0])
    weights = power(scores, top)
    total, inner = sum_of(weights), sum_of(weights * dprobs)
    for stats in known:
        factor = power(stats[0], top)
        total, inner = total + stats[1] * factor, inner + stats[2] * factor
    return weights, (top, total, inner)


def weigh_kernel(places, priors, *refs):
    q_ref, g_ref, bq_ref, bg_ref, bias_ref = refs[:5]
    blocks, before = refs[5 : 5 + len(places)], refs[5 + len(places) : 5 + len(places) + priors]
    w_ref, wb_ref, out_ref = refs[-3:]
    bias = jnp.concatenate([bias_ref[place * BLOCK : (place + 1) * BLOCK] for place in places], 0)
    wide = jnp.concatenate([bias] * 4, axis=1)
    spreads = spread_pairs(bq_ref, bg_ref)

    def products(pair, index):
        columns = columns_of(pair, index)
        if index < 0:
            (q, g), hidden = spreads[pair], bias
        else:
            q, g, hidden = q_ref[:, columns], g_ref[:, columns], wide
        key = rows_of(blocks, block_columns(pair, index, False))
        value = rows_of(blocks, block_columns(pair, index, True))
        return nt(key, q) + hidden, nt(value, g)

    def weigh(pair, index, scores, dprobs):
        weights, stats = weighed(scores, dprobs, before, pair, index)
        write_stats(out_ref, pair, index, stats)
        if index < 0:
            wb_ref[pair] = weights.astype(BF16)
        else:
            w_ref[2 * pair + index] = weights.astype(BF16)

    pipelined(units_of(q_ref), products, weigh)


def diagonal_kernel(places, priors, *refs):
    q_ref, g_ref, bq_ref, bg_ref, bias_ref = refs[:5]
    blocks, before = refs[5:7], refs[7 : 7 + priors]
    d_refs, ds_ref, dsb_ref, out_ref = refs[-5:-3], refs[-3], refs[-2], refs[-1]
    bias = jnp.concatenate([bias_ref[place * BLOCK : (place + 1) * BLOCK] for place in places], 0)
    wide = jnp.concatenate([bias] * 4, axis=1)
    spreads = spread_pairs(bq_ref, bg_ref)
    beacon = {}

    def products(pair, index):
        columns = columns_of(pair, index)
        if index < 0:
            (q, g), hidden = spreads[pair], bias
        else:
            q, g, hidden = q_ref[:, columns], g_ref[:, columns], wide
        key = rows_of(blocks, block_columns(pair, index, False))
        value = rows_of(blocks, block_columns(pair, index, True))
        return nt(key, q) + hidden, nt(value, g)

    def finish(pair, index, scores, dprobs):
        weights, stats = weighed(scores, dprobs, before, pair, index)
        write_stats(out_ref, pair, index, stats)
        _, scaled, inner = final_of(stats)
        probs = weights * scaled
        dscores = (probs * (dprobs - inner)).astype(BF16)
        store_terms(
            pair, index, probs.astype(BF16), dscores, beacon, spreads, q_ref, g_ref,
            d_refs, ds_ref, dsb_ref,
        )

    pipelined(units_of(q_ref), products, finish)


def store_terms(
    pair, index, probs, dscores, beacon, spreads, q_ref, g_ref, d_refs, ds_ref, dsb_ref
):
    if index < 0:
        qb, gb = spreads[pair]
        beacon[pair] = nn(dscores, qb), nn(probs, gb)
        dsb_ref[pair] = dscores
        return
    columns = columns_of(pair, index)
    dkey, dvalue = beacon[pair]
    ds_ref[2 * pair + index] = dscores
    head_key = ((nn(dscores, q_ref[:, columns]) + dkey[:, head(index)]) * SCALE).astype(BF16)
    head_value = (nn(probs, g_ref[:, columns]) + dvalue[:, head(index)]).astype(BF16)
    rows = head_key.shape[0] // len(d_refs)
    for place, d_ref in enumerate(d_refs):
        some = slice(place * rows, (place + 1) * rows)
        d_ref[:, block_columns(pair, index, False)] = head_key[some]
        d_ref[:, block_columns(pair, index, True)] = head_value[some]


def terms_kernel(counts, *refs):
    q_ref, g_ref, bq_ref, bg_ref, final_ref = refs[:5]
    blocks = refs[5 : 5 + sum(counts)]
    calls = refs[5 + sum(counts) : 5 + sum(counts) + 3 * len(counts)]
    d_ref, ds_ref, dsb_ref = refs[-3:]
    spreads = spread_pairs(bq_ref, bg_ref)
    beacon = {}

    def products(pair, index):
        g = spreads[pair][1] if index < 0 else g_ref[:, columns_of(pair, index)]
        return (nt(rows_of(blocks, block_columns(pair, index, True)), g),)

    def finish(pair, index, dprobs):
        top, scaled, inner = final_of(read_stats(final_ref, pair, index))
        parts = []
        for place in range(len(counts)):
            w_ref, wb_ref, st_ref = calls[3 * place : 3 * place + 3]
            weights = wb_ref[pair] if index < 0 else w_ref[2 * pair + index]
            factor = power(read_stats(st_ref, pair, index)[0], top) * scaled
            parts.append(weights.astype(F32) * factor)
        probs = jnp.concatenate(parts, axis=0)
        dscores = (probs * (dprobs - inner)).astype(BF16)
        probs = probs.astype(BF16)
        store_terms(
            pair, index, probs, dscores, beacon, spreads, q_ref, g_ref, (d_ref,), ds_ref, dsb_ref
        )

    pipelined(units_of(q_ref), products, finish)


def split_grad(weights, dprobs, stats):
    _, scaled, inner = stats
    probs = weights * scaled
    return probs.astype(BF16), (probs * (dprobs - inner)).astype(BF16)


def grads(scores, dprobs, stats):
    return split_grad(power(scores, stats[0]), dprobs, stats)


def raw_kernel(*refs):
    q_ref, k_ref, v_ref, g_ref, bq_ref, bk_ref, bv_ref, bg_ref, st_ref = refs[:9]
    far = rows_of(refs[9:17], slice(0, PAIR))
    far_ds = refs[17:20]
    far_dsb = jnp.concatenate([ref[...] for ref in refs[20:23]], axis=0)
    dq_ref, dk_ref, dv_ref, dbq_ref, own_k_ref, own_v_ref = refs[-6:]
    qb, gb = spread(bq_ref[...]), spread(bg_ref[...])
    key, value = k_ref[...], v_ref[...]
    stats = final_of(tuple(st_ref[row : row + 1, STRETCH:] for row in range(3)))
    probs, dscores = grads(nt(key, qb), nt(value, gb), stats)
    dkey, dvalue = nn(dscores, qb), nn(probs, gb)
    dqb = tn(dscores, key) + tn(far_dsb, far)
    dqb = dqb[: 2 * BEACONS]
    own_key = padded(bk_ref[...])
    probs, dscores = grads(own_mask(nt(own_key, qb)), nt(padded(bv_ref[...]), gb), stats)
    own_k_ref[...] = nn(dscores, qb)[: 2 * BEACONS] * SCALE
    own_v_ref[...] = nn(probs, gb)[: 2 * BEACONS]
    dqb = (dqb + tn(dscores, own_key)[: 2 * BEACONS]) * SCALE
    dbq_ref[:, head(0)] = dqb[:BEACONS, head(0)].astype(BF16)
    dbq_ref[:, head(1)] = dqb[BEACONS:, head(1)].astype(BF16)
    low, high = slice(0, HALF), slice(HALF, 2 * HALF)

    def products(index):
        columns = head(index)
        return raw_parts(q_ref[:, columns], key[:, columns], value[:, columns], g_ref[:, columns])

    def finish(index, p00, p01, p11):
        columns = head(index)
        q, k, g = q_ref[:, columns], key[:, columns], g_ref[:, columns]
        stats = tuple(st_ref[3 * index + row : 3 * index + row + 1, :STRETCH] for row in range(3))
        stats = final_of(stats)
        first = tuple(entry[:, low] for entry in stats)
        second = tuple(entry[:, high] for entry in stats)
        probs00, ds00 = grads(*p00, first)
        probs01, ds01 = grads(*p01, second)
        probs11, ds11 = grads(*p11, second)
        dk_ref[low, columns] = (
            (nn(ds00, q[low]) + nn(ds01, q[high]) + dkey[low, columns]) * SCALE
        ).astype(BF16)
        dk_ref[high, columns] = ((nn(ds11, q[high]) + dkey[high, columns]) * SCALE).astype(BF16)
        dv_ref[low, columns] = (
            nn(probs00, g[low]) + nn(probs01, g[high]) + dvalue[low, columns]
        ).astype(BF16)
        dv_ref[high, columns] = (nn(probs11, g[high]) + dvalue[high, columns]).astype(BF16)
        ds_far = jnp.concatenate([ref[index] for ref in far_ds], axis=0)
        dq_far = tn(far[:, columns], ds_far)
        dq_low = dq_far[:, low] + tn(k[low], ds00)
        dq_high = dq_far[:, high] + tn(k[low], ds01) + tn(k[high], ds11)
        dq_ref[low, columns] = (dq_low.T * SCALE).astype(BF16)
        dq_ref[high, columns] = (dq_high.T * SCALE).astype(BF16)

    pipelined([(0,), (1,)], products, finish)


def three(rows, start=0, pairs=1):
    return pl.BlockSpec((None, rows, PAIR * pairs), lambda step: (0, 0, start + step))


def two(rows, start=0, pairs=1):
    return pl.BlockSpec((rows, PAIR * pairs), lambda step: (0, start + step))


def paired(rows, columns, start=0, pairs=None):
    return pl.BlockSpec((pairs, rows, columns), lambda step: (start + step, 0, 0))


def shape(dims, dtype):
    return jax.ShapeDtypeStruct(dims, dtype)


def params(megabytes):
    return pltpu.CompilerParams(
        dimension_semantics=("arbitrary",), vmem_limit_bytes=megabytes * 1024 * 1024
    )


def cost(flops, moved):
    return pl.CostEstimate(flops=flops, bytes_accessed=moved, transcendentals=0)


STAT_LANES = STRETCH + LANES


def pieces(kernel, start, count, inputs, in_specs, out_specs, out_shape, before, name, flops, megabytes):
    before = tuple(before)
    aliases = {len(inputs) + place: place for place in range(len(before))}
    return pl.pallas_call(
        kernel,
        grid=(count,),
        in_specs=in_specs + [pl.BlockSpec(memory_space=pl.ANY)] * len(before),
        out_specs=out_specs,
        out_shape=out_shape,
        input_output_aliases=aliases,
        compiler_params=params(megabytes),
        cost_estimate=cost(flops, 2**10),
        name=name,
    )(*inputs, *before)


def raw_stats(start, count, inputs, before):
    raw = three(STRETCH, start)
    return pieces(
        stats_kernel,
        start, count, inputs,
        [raw] * 4 + [three(BEACONS, start)] * 4,
        [paired(8, STAT_LANES, start)],
        [shape((PAIRS, 8, STAT_LANES), F32)],
        before, f"raw_stats_{start}", 10**6, 56,
    )


def raw_grads(start, count, inputs, before):
    raw = three(STRETCH, start)
    rows = (2 * BLOCK, 3 * BLOCK, 3 * BLOCK)
    return pieces(
        raw_kernel,
        start, count, inputs,
        [raw] * 4
        + [three(BEACONS, start)] * 4
        + [paired(8, STAT_LANES, start)]
        + [pl.BlockSpec((BLOCK, 2 * PAIR), lambda step: (0, start + step))] * 8
        + [paired(count_rows, STRETCH, start, 2) for count_rows in rows]
        + [paired(count_rows, LANES, start) for count_rows in rows],
        [raw] * 3 + [three(BEACONS, start)] + [two(8, start)] * 2,
        [shape((1, STRETCH, FEAT), BF16)] * 3
        + [shape((1, BEACONS, FEAT), BF16)]
        + [shape((8, FEAT), F32)] * 2,
        before, f"raw_grads_{start}", 10**6, 16,
    )


STEP_PAIRS = 2


def block_spec(rows=BLOCK):
    return pl.BlockSpec((rows, 2 * PAIR * STEP_PAIRS), lambda step: (0, step))


def some_rows(rows, columns, per_pair, place=0):
    return pl.BlockSpec((per_pair * STEP_PAIRS, rows, columns), lambda step: (step, place, 0))


def far_call(kernel, name, inputs, in_specs, out_specs, out_shape, flops):
    shared = [three(STRETCH, 0, STEP_PAIRS)] * 2 + [three(BEACONS, 0, STEP_PAIRS)] * 2
    return pl.pallas_call(
        kernel,
        grid=(PAIRS // STEP_PAIRS,),
        in_specs=shared + in_specs,
        out_specs=out_specs,
        out_shape=out_shape,
        compiler_params=params(18),
        cost_estimate=cost(flops, 2**10),
        name=name,
    )(*inputs)


def stat_spec():
    return paired(8, STAT_LANES, 0, STEP_PAIRS)


def weigh(places, queries, bias, blocks, before):
    rows = BLOCK * len(places)
    return far_call(
        lambda *refs: weigh_kernel(places, len(before), *refs),
        "far_weights_" + "_".join(map(str, places)),
        (*queries, bias, *blocks, *before),
        [pl.BlockSpec((2 * HALF, LANES), lambda step: (0, 0))]
        + [block_spec()] * len(places)
        + [stat_spec()] * len(before),
        [some_rows(rows, STRETCH, 2), some_rows(rows, LANES, 1), stat_spec()],
        [
            shape((2 * PAIRS, rows, STRETCH), BF16),
            shape((PAIRS, rows, LANES), BF16),
            shape((PAIRS, 8, STAT_LANES), F32),
        ],
        10**6,
    )


def terms(name, queries, final, blocks, calls):
    counts = tuple(count for _, count, _ in calls)
    rows = BLOCK * sum(counts)
    call_specs, call_inputs = [], []
    for outputs, count, place in calls:
        call_specs += [
            some_rows(BLOCK * count, STRETCH, 2, place),
            some_rows(BLOCK * count, LANES, 1, place),
            stat_spec(),
        ]
        call_inputs += list(outputs)
    return far_call(
        lambda *refs: terms_kernel(counts, *refs),
        name,
        (*queries, final, *blocks, *call_inputs),
        [stat_spec()] + [block_spec()] * len(blocks) + call_specs,
        [block_spec(rows), some_rows(rows, STRETCH, 2), some_rows(rows, LANES, 1)],
        [
            shape((rows, 2 * FEAT), BF16),
            shape((2 * PAIRS, rows, STRETCH), BF16),
            shape((PAIRS, rows, LANES), BF16),
        ],
        10**6,
    )


def diagonal_terms(queries, bias, blocks, before):
    rows = 2 * BLOCK
    return far_call(
        lambda *refs: diagonal_kernel((3, 7), len(before), *refs),
        "far_diagonal",
        (*queries, bias, *blocks, *before),
        [pl.BlockSpec((2 * HALF, LANES), lambda step: (0, 0))]
        + [block_spec()] * 2
        + [stat_spec()] * len(before),
        [block_spec()] * 2 + [some_rows(rows, STRETCH, 2), some_rows(rows, LANES, 1), stat_spec()],
        [shape((BLOCK, 2 * FEAT), BF16)] * 2
        + [
            shape((2 * PAIRS, rows, STRETCH), BF16),
            shape((PAIRS, rows, LANES), BF16),
            shape((PAIRS, 8, STAT_LANES), F32),
        ],
        10**6,
    )


def woven(key, value):
    parts = [rows.reshape(BEACONS, PAIRS, 1, PAIR) for rows in (key, value)]
    return jnp.concatenate(parts, axis=2).reshape(BEACONS, 2 * FEAT)


def unwoven(both):
    parts = both.reshape(BEACONS, PAIRS, 2, PAIR)
    return parts[:, :, 0].reshape(BEACONS, FEAT), parts[:, :, 1].reshape(BEACONS, FEAT)


def on_device(
    raw_q, raw_k, raw_v, raw_grad, beacon_q, beacon_k, beacon_v, beacon_grad, assign, prefix
):
    raw = (raw_q, raw_k, raw_v, raw_grad)
    rest = (beacon_k, beacon_v, beacon_grad)

    def raw_stats_of(place, count, token, stats):
        return raw_stats(place, count, (*raw, token, *rest), stats)

    def queries(token):
        return raw_q, raw_grad, token, beacon_grad

    own0 = lax.optimization_barrier(woven(beacon_k[0], beacon_v[0]))
    (got, bias) = beside(
        own0, assign, lambda value, token: (exchange(value, 0), far_bias(token, prefix))
    )
    own0 = joined(own0, got)
    stats = ()
    for step, place, count in ((1, 0, 1), (2, 1, 1), (3, 2, 2)):
        got, stats = beside(
            own0,
            (beacon_q, stats),
            lambda value, token, step=step, place=place, count=count: (
                exchange(value, step), raw_stats_of(place, count, *token)
            ),
        )
        own0 = joined(own0, got)

    def stage_one(value, token):
        got = exchange(value, 4), exchange(value, 5), swap(value)
        stats = raw_stats_of(4, 4, *token)
        late, token, stats = lax.optimization_barrier((got[2], token[0], stats))
        return got, stats, weigh((0, 4), queries(token), bias, (value, late), ())

    (own_u, own_v, other0), stats, first = beside(own0, (beacon_q, stats), stage_one)

    def stage_two(values, token):
        own_u, own_v = values
        got = exchange(own_v[:, :FEAT], 4), exchange(own_u[:, FEAT:], 5)
        others = swap(own_u), swap(own_v)
        blocks = (own_u, own_v, *others)
        return got, others, weigh((1, 2, 5, 6), queries(token), bias, blocks, first[2:])

    (got_low, got_high), (other_u, other_v), second = beside((own_u, own_v), beacon_q, stage_two)
    own_uv = joined(got_low, got_high, axis=1)
    other_uv = swap(own_uv)
    d_own, d_other, ds_uv, dsb_uv, final = diagonal_terms(
        queries(beacon_q), bias, (own_uv, other_uv), (second[2], *stats)
    )
    got, others = beside(
        d_other,
        beacon_q,
        lambda value, token: (
            swap(value),
            terms(
                "other_rest", queries(token), final, (other0, other_u, other_v),
                [(first, 1, 1), (second, 2, 1)],
            ),
        ),
    )
    diagonal = added(d_own, got)

    def back_two(values, token):
        value, rest = values
        got = exchange(value[:, :FEAT], 4), exchange(value[:, FEAT:], 5)
        return got, swap(rest), terms(
            "own_rest", queries(token), final, (own0, own_u, own_v),
            [(first, 1, 0), (second, 2, 0)],
        )

    (got_low, got_high), got, owns = beside((diagonal, others[0]), beacon_q, back_two)
    blocks = [slice(place * BLOCK, (place + 1) * BLOCK) for place in range(3)]
    sums = [(owns[0][rows], got[rows]) for rows in blocks]
    none = jnp.zeros((BLOCK, FEAT), BF16)
    total = added(*sums[0])
    total_u = added(*sums[1], jnp.concatenate([none, got_high], axis=1))
    total_v = added(*sums[2], jnp.concatenate([got_low, none], axis=1))
    known = (
        final, own_uv, other_uv, other0, other_u, other_v, own0, own_u, own_v,
        ds_uv, others[1], owns[1], dsb_uv, others[2], owns[2],
    )

    def raw_grads_of(place, count, token, outs):
        return raw_grads(place, count, (*raw, token, *rest, *known), outs)

    (got_u, got_v), outs = beside(
        (total_u, total_v),
        beacon_q,
        lambda values, token: (
            (exchange(values[0], 4), exchange(values[1], 5)), raw_grads_of(0, 3, token, ())
        ),
    )
    total = added(total, got_u, got_v)
    for step, place, count in ((3, 3, 2), (2, 5, 1), (1, 6, 1), (0, 7, 1)):
        half = total.shape[0] // 2
        got, outs = beside(
            total[half:],
            (beacon_q, outs),
            lambda value, token, step=step, place=place, count=count: (
                exchange(value, step), raw_grads_of(place, count, *token)
            ),
        )
        kept = total[:half]
        if step:
            total = added(kept, got)
    raw_dq, raw_dk, raw_dv, beacon_dq, own_dk, own_dv = outs
    total_k, total_v = unwoven(kept.astype(F32) + got.astype(F32))
    beacon_dk = (own_dk[:BEACONS] + total_k).astype(BF16)[None]
    beacon_dv = (own_dv[:BEACONS] + total_v).astype(BF16)[None]
    return (raw_dq, raw_dk, raw_dv, beacon_dq, beacon_dk, beacon_dv)


def solution(mesh):
    named = Mesh(mesh.devices.reshape(SIZES), NAMES)
    placed = P(NAMES, None, None)
    return jax.shard_map(
        on_device,
        mesh=named,
        in_specs=(placed,) * 8 + (P(), P()),
        out_specs=(placed,) * 6,
        check_vma=False,
    )
```

```python
import math

import jax
import jax.numpy as jnp
import numpy as np
from jax import lax
from jax.experimental import pallas as pl
from jax.experimental.pallas import tpu as pltpu
from jax.sharding import Mesh
from jax.sharding import PartitionSpec as P

HEAD_DIM = 128
PAIR = 2 * HEAD_DIM
BEACONS = 4
STRETCH = 512
FEAT = 2048
PAIRS = FEAT // PAIR
LANES = 128
HALF = 256
BLOCK = 64
SCALE = HEAD_DIM ** (-0.5)
LOG_SCALE = SCALE * math.log2(math.e)
HIDDEN = -1e30
F32 = jnp.float32
BF16 = jnp.bfloat16

NAMES = ("x_lo", "z", "core", "y", "x_hi")
SIZES = (2, 4, 2, 4, 2)

X0, X1, Y0, Y1, Z0, Z1 = 1, 2, 4, 8, 16, 32
STEPS = ((Z0, Z1, Y0, Y1, X0, X1), (X0, X1, Z0, Z1, Y0, Y1))


def gray(position):
    return position ^ (position >> 1)


def slot_of(label, core):
    x, y, z = (gray((label >> shift) & 3) for shift in (0, 2, 4))
    return ((((x & 1) * 4 + z) * 2 + core) * 4 + y) * 2 + (x >> 1)


def exchange(value, step):
    pairs = []
    for label in range(64):
        for core in range(2):
            partner = label ^ STEPS[core][step]
            pairs.append((slot_of(label, core), slot_of(partner, core)))
    return lax.ppermute(value, NAMES, sorted(pairs))


def swap(value):
    return lax.ppermute(value, "core", [(0, 1), (1, 0)])


def beside(values, token, work):
    values, token = lax.optimization_barrier((values, token))
    return lax.optimization_barrier(work(values, token))


def joined(kept, got, axis=0):
    return lax.optimization_barrier(jnp.concatenate([kept, got], axis=axis))


def added(first, *more):
    total = first.astype(F32)
    for term in more:
        total = total + term.astype(F32)
    return total.astype(BF16)


def mask_kernel(assign_ref, prefix_ref, bias_ref):
    x_lo, z, core, y, x_hi = (lax.axis_index(name) for name in NAMES)
    mine = gray(x_hi * 2 + x_lo) | (gray(y) << 2) | (gray(z) << 4)
    own = slot_of(mine, core)
    numbers = lax.broadcasted_iota(jnp.int32, (1, LANES), 1)
    assign, prefix = assign_ref[...], prefix_ref[...]

    def pick(values, index):
        return jnp.sum(jnp.where(numbers == index, values, 0).astype(F32), axis=1, keepdims=True)

    stretch = pick(assign, own).astype(jnp.int32)
    lowest = stretch - pick(prefix, stretch).astype(jnp.int32)
    seen = jnp.where((assign >= lowest) & (assign < stretch), 1.0, 0.0)
    place = lax.broadcasted_iota(jnp.int32, (HALF, LANES), 0) >> 2
    labels = []
    for steps in STEPS:
        label = jnp.full((HALF, LANES), mine, jnp.int32)
        for step, bit in enumerate(steps):
            label = label ^ (((place >> step) & 1) * bit)
        labels.append(label)
    for half in range(2):
        label = jnp.where(core == half, labels[0], labels[1])
        slots = slot_of(label, core if half == 0 else 1 - core)
        found = jnp.sum(jnp.where(slots == numbers, seen, 0.0), axis=1, keepdims=True)
        rows = slice(half * HALF, (half + 1) * HALF)
        bias_ref[rows] = jnp.broadcast_to(jnp.where(found > 0.5, 0.0, HIDDEN), (HALF, LANES))


def far_bias(assign, prefix):
    line = pl.BlockSpec((1, LANES), lambda: (0, 0))
    return pl.pallas_call(
        mask_kernel,
        in_specs=[line, line],
        out_specs=pl.BlockSpec((2 * HALF, LANES), lambda: (0, 0)),
        out_shape=jax.ShapeDtypeStruct((2 * HALF, LANES), F32),
        name="far_mask",
    )(assign.reshape(1, LANES), prefix.reshape(1, LANES))


def spread(rows):
    twice = jnp.concatenate([rows.astype(F32)] * 2, axis=0)
    row = lax.broadcasted_iota(jnp.int32, twice.shape, 0)
    column = lax.broadcasted_iota(jnp.int32, twice.shape, 1)
    kept = jnp.where((row < BEACONS) == (column < HEAD_DIM), twice, 0.0)
    rest = jnp.zeros((LANES - 2 * BEACONS, rows.shape[1]), F32)
    return jnp.concatenate([kept, rest], axis=0).astype(BF16)


def padded(rows):
    rest = jnp.zeros((12, rows.shape[1]), F32)
    return jnp.concatenate([rows.astype(F32), rest], axis=0).astype(BF16)


def nt(a, b):
    return lax.dot_general(a, b, (((1,), (1,)), ((), ())), preferred_element_type=F32)


def nn(a, b):
    return lax.dot_general(a, b, (((1,), (0,)), ((), ())), preferred_element_type=F32)


def tn(a, b):
    return lax.dot_general(a, b, (((0,), (0,)), ((), ())), preferred_element_type=F32)


def top_of(scores):
    return jnp.max(scores, axis=0, keepdims=True)


def sum_of(values):
    return jnp.sum(values, axis=0, keepdims=True)


def causal(scores):
    rows = lax.broadcasted_iota(jnp.int32, scores.shape, 0)
    columns = lax.broadcasted_iota(jnp.int32, scores.shape, 1)
    return jnp.where(rows <= columns, scores, HIDDEN)


def own_mask(scores):
    rows = lax.broadcasted_iota(jnp.int32, scores.shape, 0)
    columns = lax.broadcasted_iota(jnp.int32, scores.shape, 1)
    return jnp.where((rows <= (columns & 3)) & (rows < BEACONS), scores, HIDDEN)


def power(scores, top):
    return jnp.exp2((scores - top) * LOG_SCALE)


def stats_of(parts):
    top = top_of(parts[0][0])
    for scores, _ in parts[1:]:
        top = jnp.maximum(top, top_of(scores))
    total = inner = None
    for scores, dprobs in parts:
        weights = power(scores, top)
        part, part_inner = sum_of(weights), sum_of(weights * dprobs)
        total = part if total is None else total + part
        inner = part_inner if inner is None else inner + part_inner
    return top, total, inner


def head(index):
    return slice(index * HEAD_DIM, (index + 1) * HEAD_DIM)


def raw_parts(q, k, v, g):
    low, high = slice(0, HALF), slice(HALF, 2 * HALF)
    s00 = causal(nt(k[low], q[low]))
    s01 = nt(k[low], q[high])
    s11 = causal(nt(k[high], q[high]))
    d00 = nt(v[low], g[low])
    d01 = nt(v[low], g[high])
    d11 = nt(v[high], g[high])
    return (s00, d00), (s01, d01), (s11, d11)


def stats_kernel(q_ref, k_ref, v_ref, g_ref, bq_ref, bk_ref, bv_ref, bg_ref, *refs):
    st_ref = refs[-1]
    qb, gb = spread(bq_ref[...]), spread(bg_ref[...])

    def products(index):
        if index < 0:
            raw = nt(k_ref[...], qb), nt(v_ref[...], gb)
            return raw, (own_mask(nt(padded(bk_ref[...]), qb)), nt(padded(bv_ref[...]), gb))
        columns = head(index)
        return raw_parts(
            q_ref[:, columns], k_ref[:, columns], v_ref[:, columns], g_ref[:, columns]
        )

    def store(index, *parts):
        if index < 0:
            found = ((STRETCH, LANES, stats_of(parts)),)
        else:
            p00, p01, p11 = parts
            found = ((0, HALF, stats_of([p00])), (HALF, HALF, stats_of([p01, p11])))
        for place, width, stats in found:
            for row, entry in enumerate(stats):
                row += 3 * max(index, 0)
                st_ref[row : row + 1, place : place + width] = entry

    pipelined([(-1,), (0,), (1,)], products, store)


def units_of(q_ref):
    return [(pair, index) for pair in range(q_ref.shape[1] // PAIR) for index in (-1, 0, 1)]


def columns_of(pair, index):
    if index < 0:
        return slice(pair * PAIR, (pair + 1) * PAIR)
    return head(2 * pair + index)


def block_columns(pair, index, value):
    start = 2 * pair * PAIR + (PAIR if value else 0)
    if index < 0:
        return slice(start, start + PAIR)
    return slice(start + index * HEAD_DIM, start + (index + 1) * HEAD_DIM)


def lanes_of(index):
    return slice(STRETCH, STAT_LANES) if index < 0 else slice(0, STRETCH)


def read_stats(ref, pair, index):
    base = 3 * max(index, 0)
    return tuple(ref[pair, base + row : base + row + 1, lanes_of(index)] for row in range(3))


def write_stats(ref, pair, index, stats):
    base = 3 * max(index, 0)
    for row, entry in enumerate(stats):
        ref[pair, base + row : base + row + 1, lanes_of(index)] = entry


def final_of(stats):
    top, total, inner = stats
    scaled = 1.0 / total
    return top, scaled, inner * scaled


def spread_pairs(*refs):
    pairs = refs[0].shape[1] // PAIR
    return [
        [spread(ref[:, pair * PAIR : (pair + 1) * PAIR]) for ref in refs] for pair in range(pairs)
    ]


def rows_of(refs, columns):
    return jnp.concatenate([ref[:, columns] for ref in refs], axis=0)


def pipelined(units, first, second):
    ready = first(*units[0])
    for place, unit in enumerate(units):
        now = ready
        if place + 1 < len(units):
            ready = first(*units[place + 1])
        second(*unit, *now)


def weighed(scores, dprobs, before, pair, index):
    known = [read_stats(ref, pair, index) for ref in before]
    top = top_of(scores)
    for stats in known:
        top = jnp.maximum(top, stats[0])
    weights = power(scores, top)
    total, inner = sum_of(weights), sum_of(weights * dprobs)
    for stats in known:
        factor = power(stats[0], top)
        total, inner = total + stats[1] * factor, inner + stats[2] * factor
    return weights, (top, total, inner)


def weigh_kernel(places, priors, *refs):
    q_ref, g_ref, bq_ref, bg_ref, bias_ref = refs[:5]
    blocks, before = refs[5 : 5 + len(places)], refs[5 + len(places) : 5 + len(places) + priors]
    w_ref, wb_ref, dp_ref, dpb_ref, out_ref = refs[-5:]
    bias = jnp.concatenate([bias_ref[place * BLOCK : (place + 1) * BLOCK] for place in places], 0)
    wide = jnp.concatenate([bias] * 4, axis=1)
    spreads = spread_pairs(bq_ref, bg_ref)

    def products(pair, index):
        columns = columns_of(pair, index)
        if index < 0:
            (q, g), hidden = spreads[pair], bias
        else:
            q, g, hidden = q_ref[:, columns], g_ref[:, columns], wide
        key = rows_of(blocks, block_columns(pair, index, False))
        value = rows_of(blocks, block_columns(pair, index, True))
        return nt(key, q) + hidden, nt(value, g)

    def weigh(pair, index, scores, dprobs):
        kept = dprobs.astype(BF16)
        weights, stats = weighed(scores, kept.astype(F32), before, pair, index)
        write_stats(out_ref, pair, index, stats)
        if index < 0:
            wb_ref[pair], dpb_ref[pair] = weights.astype(BF16), kept
        else:
            w_ref[2 * pair + index], dp_ref[2 * pair + index] = weights.astype(BF16), kept

    pipelined(units_of(q_ref), products, weigh)


def diagonal_kernel(places, priors, *refs):
    q_ref, g_ref, bq_ref, bg_ref, bias_ref = refs[:5]
    blocks, before = refs[5:7], refs[7 : 7 + priors]
    d_refs, ds_ref, dsb_ref, out_ref = refs[-5:-3], refs[-3], refs[-2], refs[-1]
    bias = jnp.concatenate([bias_ref[place * BLOCK : (place + 1) * BLOCK] for place in places], 0)
    wide = jnp.concatenate([bias] * 4, axis=1)
    spreads = spread_pairs(bq_ref, bg_ref)
    beacon = {}

    def products(pair, index):
        columns = columns_of(pair, index)
        if index < 0:
            (q, g), hidden = spreads[pair], bias
        else:
            q, g, hidden = q_ref[:, columns], g_ref[:, columns], wide
        key = rows_of(blocks, block_columns(pair, index, False))
        value = rows_of(blocks, block_columns(pair, index, True))
        return nt(key, q) + hidden, nt(value, g)

    def finish(pair, index, scores, dprobs):
        weights, stats = weighed(scores, dprobs, before, pair, index)
        write_stats(out_ref, pair, index, stats)
        _, scaled, inner = final_of(stats)
        probs = weights * scaled
        dscores = (probs * (dprobs - inner)).astype(BF16)
        store_terms(
            pair, index, probs.astype(BF16), dscores, beacon, spreads, q_ref, g_ref,
            d_refs, ds_ref, dsb_ref,
        )

    pipelined(units_of(q_ref), products, finish)


def store_terms(
    pair, index, probs, dscores, beacon, spreads, q_ref, g_ref, d_refs, ds_ref, dsb_ref
):
    if index < 0:
        qb, gb = spreads[pair]
        beacon[pair] = nn(dscores, qb), nn(probs, gb)
        dsb_ref[pair] = dscores
        return
    columns = columns_of(pair, index)
    dkey, dvalue = beacon[pair]
    ds_ref[2 * pair + index] = dscores
    head_key = ((nn(dscores, q_ref[:, columns]) + dkey[:, head(index)]) * SCALE).astype(BF16)
    head_value = (nn(probs, g_ref[:, columns]) + dvalue[:, head(index)]).astype(BF16)
    rows = head_key.shape[0] // len(d_refs)
    for place, d_ref in enumerate(d_refs):
        some = slice(place * rows, (place + 1) * rows)
        d_ref[:, block_columns(pair, index, False)] = head_key[some]
        d_ref[:, block_columns(pair, index, True)] = head_value[some]


def terms_kernel(counts, *refs):
    q_ref, g_ref, bq_ref, bg_ref, final_ref = refs[:5]
    calls = refs[5 : 5 + 5 * len(counts)]
    d_ref, ds_ref, dsb_ref = refs[-3:]
    spreads = spread_pairs(bq_ref, bg_ref)
    beacon = {}

    def products(pair, index):
        return ()

    def finish(pair, index):
        top, scaled, inner = final_of(read_stats(final_ref, pair, index))
        parts, dprobs = [], []
        for place in range(len(counts)):
            w_ref, wb_ref, dp_ref, dpb_ref, st_ref = calls[5 * place : 5 * place + 5]
            weights = wb_ref[pair] if index < 0 else w_ref[2 * pair + index]
            kept = dpb_ref[pair] if index < 0 else dp_ref[2 * pair + index]
            factor = power(read_stats(st_ref, pair, index)[0], top) * scaled
            parts.append(weights.astype(F32) * factor)
            dprobs.append(kept.astype(F32))
        probs, dprobs = jnp.concatenate(parts, axis=0), jnp.concatenate(dprobs, axis=0)
        dscores = (probs * (dprobs - inner)).astype(BF16)
        probs = probs.astype(BF16)
        store_terms(
            pair, index, probs, dscores, beacon, spreads, q_ref, g_ref, (d_ref,), ds_ref, dsb_ref
        )

    pipelined(units_of(q_ref), products, finish)


def split_grad(weights, dprobs, stats):
    _, scaled, inner = stats
    probs = weights * scaled
    return probs.astype(BF16), (probs * (dprobs - inner)).astype(BF16)


def grads(scores, dprobs, stats):
    return split_grad(power(scores, stats[0]), dprobs, stats)


def raw_kernel(*refs):
    q_ref, k_ref, v_ref, g_ref, bq_ref, bk_ref, bv_ref, bg_ref, st_ref = refs[:9]
    far = rows_of(refs[9:17], slice(0, PAIR))
    far_ds = refs[17:20]
    far_dsb = jnp.concatenate([ref[...] for ref in refs[20:23]], axis=0)
    dq_ref, dk_ref, dv_ref, dbq_ref, own_k_ref, own_v_ref = refs[-6:]
    qb, gb = spread(bq_ref[...]), spread(bg_ref[...])
    key, value = k_ref[...], v_ref[...]
    stats = final_of(tuple(st_ref[row : row + 1, STRETCH:] for row in range(3)))
    probs, dscores = grads(nt(key, qb), nt(value, gb), stats)
    dkey, dvalue = nn(dscores, qb), nn(probs, gb)
    dqb = tn(dscores, key) + tn(far_dsb, far)
    dqb = dqb[: 2 * BEACONS]
    own_key = padded(bk_ref[...])
    probs, dscores = grads(own_mask(nt(own_key, qb)), nt(padded(bv_ref[...]), gb), stats)
    own_k_ref[...] = nn(dscores, qb)[: 2 * BEACONS] * SCALE
    own_v_ref[...] = nn(probs, gb)[: 2 * BEACONS]
    dqb = (dqb + tn(dscores, own_key)[: 2 * BEACONS]) * SCALE
    dbq_ref[:, head(0)] = dqb[:BEACONS, head(0)].astype(BF16)
    dbq_ref[:, head(1)] = dqb[BEACONS:, head(1)].astype(BF16)
    low, high = slice(0, HALF), slice(HALF, 2 * HALF)

    def products(index):
        columns = head(index)
        return raw_parts(q_ref[:, columns], key[:, columns], value[:, columns], g_ref[:, columns])

    def finish(index, p00, p01, p11):
        columns = head(index)
        q, k, g = q_ref[:, columns], key[:, columns], g_ref[:, columns]
        stats = tuple(st_ref[3 * index + row : 3 * index + row + 1, :STRETCH] for row in range(3))
        stats = final_of(stats)
        first = tuple(entry[:, low] for entry in stats)
        second = tuple(entry[:, high] for entry in stats)
        probs00, ds00 = grads(*p00, first)
        probs01, ds01 = grads(*p01, second)
        probs11, ds11 = grads(*p11, second)
        dk_ref[low, columns] = (
            (nn(ds00, q[low]) + nn(ds01, q[high]) + dkey[low, columns]) * SCALE
        ).astype(BF16)
        dk_ref[high, columns] = ((nn(ds11, q[high]) + dkey[high, columns]) * SCALE).astype(BF16)
        dv_ref[low, columns] = (
            nn(probs00, g[low]) + nn(probs01, g[high]) + dvalue[low, columns]
        ).astype(BF16)
        dv_ref[high, columns] = (nn(probs11, g[high]) + dvalue[high, columns]).astype(BF16)
        ds_far = jnp.concatenate([ref[index] for ref in far_ds], axis=0)
        dq_far = tn(far[:, columns], ds_far)
        dq_low = dq_far[:, low] + tn(k[low], ds00)
        dq_high = dq_far[:, high] + tn(k[low], ds01) + tn(k[high], ds11)
        dq_ref[low, columns] = (dq_low.T * SCALE).astype(BF16)
        dq_ref[high, columns] = (dq_high.T * SCALE).astype(BF16)

    pipelined([(0,), (1,)], products, finish)


def three(rows, start=0, pairs=1):
    return pl.BlockSpec((None, rows, PAIR * pairs), lambda step: (0, 0, start + step))


def two(rows, start=0, pairs=1):
    return pl.BlockSpec((rows, PAIR * pairs), lambda step: (0, start + step))


def paired(rows, columns, start=0, pairs=None):
    return pl.BlockSpec((pairs, rows, columns), lambda step: (start + step, 0, 0))


def shape(dims, dtype):
    return jax.ShapeDtypeStruct(dims, dtype)


def params(megabytes):
    return pltpu.CompilerParams(
        dimension_semantics=("arbitrary",), vmem_limit_bytes=megabytes * 1024 * 1024
    )


def cost(flops, moved):
    return pl.CostEstimate(flops=flops, bytes_accessed=moved, transcendentals=0)


STAT_LANES = STRETCH + LANES


def pieces(kernel, start, count, inputs, in_specs, out_specs, out_shape, before, name, flops, megabytes):
    before = tuple(before)
    aliases = {len(inputs) + place: place for place in range(len(before))}
    return pl.pallas_call(
        kernel,
        grid=(count,),
        in_specs=in_specs + [pl.BlockSpec(memory_space=pl.ANY)] * len(before),
        out_specs=out_specs,
        out_shape=out_shape,
        input_output_aliases=aliases,
        compiler_params=params(megabytes),
        cost_estimate=cost(flops, 2**10),
        name=name,
    )(*inputs, *before)


def raw_stats(start, count, inputs, before):
    raw = three(STRETCH, start)
    return pieces(
        stats_kernel,
        start, count, inputs,
        [raw] * 4 + [three(BEACONS, start)] * 4,
        [paired(8, STAT_LANES, start)],
        [shape((PAIRS, 8, STAT_LANES), F32)],
        before, f"raw_stats_{start}", 10**6, 56,
    )


def raw_grads(start, count, inputs, before):
    raw = three(STRETCH, start)
    rows = (2 * BLOCK, 3 * BLOCK, 3 * BLOCK)
    return pieces(
        raw_kernel,
        start, count, inputs,
        [raw] * 4
        + [three(BEACONS, start)] * 4
        + [paired(8, STAT_LANES, start)]
        + [pl.BlockSpec((BLOCK, 2 * PAIR), lambda step: (0, start + step))] * 8
        + [paired(count_rows, STRETCH, start, 2) for count_rows in rows]
        + [paired(count_rows, LANES, start) for count_rows in rows],
        [raw] * 3 + [three(BEACONS, start)] + [two(8, start)] * 2,
        [shape((1, STRETCH, FEAT), BF16)] * 3
        + [shape((1, BEACONS, FEAT), BF16)]
        + [shape((8, FEAT), F32)] * 2,
        before, f"raw_grads_{start}", 10**6, 16,
    )


STEP_PAIRS = 2


def block_spec(rows=BLOCK):
    return pl.BlockSpec((rows, 2 * PAIR * STEP_PAIRS), lambda step: (0, step))


def some_rows(rows, columns, per_pair, place=0):
    return pl.BlockSpec((per_pair * STEP_PAIRS, rows, columns), lambda step: (step, place, 0))


def far_call(kernel, name, inputs, in_specs, out_specs, out_shape, flops):
    shared = [three(STRETCH, 0, STEP_PAIRS)] * 2 + [three(BEACONS, 0, STEP_PAIRS)] * 2
    return pl.pallas_call(
        kernel,
        grid=(PAIRS // STEP_PAIRS,),
        in_specs=shared + in_specs,
        out_specs=out_specs,
        out_shape=out_shape,
        compiler_params=params(12),
        cost_estimate=cost(flops, 2**10),
        name=name,
    )(*inputs)


def stat_spec():
    return paired(8, STAT_LANES, 0, STEP_PAIRS)


def weigh(places, queries, bias, blocks, before):
    rows = BLOCK * len(places)
    return far_call(
        lambda *refs: weigh_kernel(places, len(before), *refs),
        "far_weights_" + "_".join(map(str, places)),
        (*queries, bias, *blocks, *before),
        [pl.BlockSpec((2 * HALF, LANES), lambda step: (0, 0))]
        + [block_spec()] * len(places)
        + [stat_spec()] * len(before),
        [some_rows(rows, STRETCH, 2), some_rows(rows, LANES, 1)] * 2 + [stat_spec()],
        [shape((2 * PAIRS, rows, STRETCH), BF16), shape((PAIRS, rows, LANES), BF16)] * 2
        + [shape((PAIRS, 8, STAT_LANES), F32)],
        10**6,
    )


def terms(name, queries, final, calls):
    counts = tuple(count for _, count, _ in calls)
    rows = BLOCK * sum(counts)
    call_specs, call_inputs = [], []
    for outputs, count, place in calls:
        call_specs += [
            *[
                some_rows(BLOCK * count, STRETCH, 2, place),
                some_rows(BLOCK * count, LANES, 1, place),
            ]
            * 2,
            stat_spec(),
        ]
        call_inputs += list(outputs)
    return far_call(
        lambda *refs: terms_kernel(counts, *refs),
        name,
        (*queries, final, *call_inputs),
        [stat_spec()] + call_specs,
        [block_spec(rows), some_rows(rows, STRETCH, 2), some_rows(rows, LANES, 1)],
        [
            shape((rows, 2 * FEAT), BF16),
            shape((2 * PAIRS, rows, STRETCH), BF16),
            shape((PAIRS, rows, LANES), BF16),
        ],
        10**6,
    )


def diagonal_terms(queries, bias, blocks, before):
    rows = 2 * BLOCK
    return far_call(
        lambda *refs: diagonal_kernel((3, 7), len(before), *refs),
        "far_diagonal",
        (*queries, bias, *blocks, *before),
        [pl.BlockSpec((2 * HALF, LANES), lambda step: (0, 0))]
        + [block_spec()] * 2
        + [stat_spec()] * len(before),
        [block_spec()] * 2 + [some_rows(rows, STRETCH, 2), some_rows(rows, LANES, 1), stat_spec()],
        [shape((BLOCK, 2 * FEAT), BF16)] * 2
        + [
            shape((2 * PAIRS, rows, STRETCH), BF16),
            shape((PAIRS, rows, LANES), BF16),
            shape((PAIRS, 8, STAT_LANES), F32),
        ],
        10**6,
    )


def woven(both):
    parts = both.reshape(both.shape[0], 2, PAIRS, PAIR)
    return lax.optimization_barrier(parts.transpose(0, 2, 1, 3).reshape(both.shape))


def unwoven(both):
    parts = both.reshape(BEACONS, PAIRS, 2, PAIR)
    return parts[:, :, 0].reshape(BEACONS, FEAT), parts[:, :, 1].reshape(BEACONS, FEAT)


def on_device(
    raw_q, raw_k, raw_v, raw_grad, beacon_q, beacon_k, beacon_v, beacon_grad, assign, prefix
):
    raw = (raw_q, raw_k, raw_v, raw_grad)
    rest = (beacon_k, beacon_v, beacon_grad)

    def raw_stats_of(place, count, token, stats):
        return raw_stats(place, count, (*raw, token, *rest), stats)

    def queries(token):
        return raw_q, raw_grad, token, beacon_grad

    own0 = lax.optimization_barrier(jnp.concatenate([beacon_k[0], beacon_v[0]], axis=1))
    (got, bias) = beside(
        own0, assign, lambda value, token: (exchange(value, 0), far_bias(token, prefix))
    )
    own0 = woven(joined(own0, got))
    stats = ()
    for step, place, count in ((1, 0, 1), (2, 1, 1), (3, 2, 3)):
        got, stats = beside(
            own0,
            (beacon_q, stats),
            lambda value, token, step=step, place=place, count=count: (
                exchange(value, step), raw_stats_of(place, count, *token)
            ),
        )
        own0 = joined(own0, got)

    def stage_one(value, token):
        got = exchange(value, 4), exchange(value, 5), swap(value)
        stats = raw_stats_of(5, 3, *token)
        late, token, stats = lax.optimization_barrier((got[2], token[0], stats))
        return got, stats, weigh((0, 4), queries(token), bias, (value, late), ())

    (own_u, own_v, other0), stats, first = beside(own0, (beacon_q, stats), stage_one)

    def stage_two(values, token):
        own_u, own_v = values
        got = exchange(own_v[:, :FEAT], 4), exchange(own_u[:, FEAT:], 5)
        others = swap(own_u), swap(own_v)
        blocks = (own_u, own_v, *others)
        return got, others, weigh((1, 2, 5, 6), queries(token), bias, blocks, first[4:])

    (got_low, got_high), (other_u, other_v), second = beside((own_u, own_v), beacon_q, stage_two)
    own_uv = joined(got_low, got_high, axis=1)
    other_uv = swap(own_uv)
    d_own, d_other, ds_uv, dsb_uv, final = diagonal_terms(
        queries(beacon_q), bias, (own_uv, other_uv), (second[4], *stats)
    )
    got, others = beside(
        d_other,
        beacon_q,
        lambda value, token: (
            swap(value),
            terms(
                "other_rest", queries(token), final,
                [(first, 1, 1), (second, 2, 1)],
            ),
        ),
    )
    diagonal = added(d_own, got)

    def back_two(values, token):
        value, rest = values
        got = exchange(value[:, :FEAT], 4), exchange(value[:, FEAT:], 5)
        return got, swap(rest), terms(
            "own_rest", queries(token), final,
            [(first, 1, 0), (second, 2, 0)],
        )

    (got_low, got_high), got, owns = beside((diagonal, others[0]), beacon_q, back_two)
    blocks = [slice(place * BLOCK, (place + 1) * BLOCK) for place in range(3)]
    sums = [(owns[0][rows], got[rows]) for rows in blocks]
    none = jnp.zeros((BLOCK, FEAT), BF16)
    total = added(*sums[0])
    total_u = added(*sums[1], jnp.concatenate([none, got_high], axis=1))
    total_v = added(*sums[2], jnp.concatenate([got_low, none], axis=1))
    known = (
        final, own_uv, other_uv, other0, other_u, other_v, own0, own_u, own_v,
        ds_uv, others[1], owns[1], dsb_uv, others[2], owns[2],
    )

    def raw_grads_of(place, count, token, outs):
        return raw_grads(place, count, (*raw, token, *rest, *known), outs)

    (got_u, got_v), outs = beside(
        (total_u, total_v),
        beacon_q,
        lambda values, token: (
            (exchange(values[0], 4), exchange(values[1], 5)), raw_grads_of(0, 3, token, ())
        ),
    )
    total = added(total, got_u, got_v)
    for step, place, count in ((3, 3, 2), (2, 5, 1), (1, 6, 1), (0, 7, 1)):
        half = total.shape[0] // 2
        got, outs = beside(
            total[half:],
            (beacon_q, outs),
            lambda value, token, step=step, place=place, count=count: (
                exchange(value, step), raw_grads_of(place, count, *token)
            ),
        )
        kept = total[:half]
        if step:
            total = added(kept, got)
    raw_dq, raw_dk, raw_dv, beacon_dq, own_dk, own_dv = outs
    total_k, total_v = unwoven(kept.astype(F32) + got.astype(F32))
    beacon_dk = (own_dk[:BEACONS] + total_k).astype(BF16)[None]
    beacon_dv = (own_dv[:BEACONS] + total_v).astype(BF16)[None]
    return (raw_dq, raw_dk, raw_dv, beacon_dq, beacon_dk, beacon_dv)


def solution(mesh):
    named = Mesh(mesh.devices.reshape(SIZES), NAMES)
    placed = P(NAMES, None, None)
    return jax.shard_map(
        on_device,
        mesh=named,
        in_specs=(placed,) * 8 + (P(), P()),
        out_specs=(placed,) * 6,
        check_vma=False,
    )
```

```python
import math

import jax
import jax.numpy as jnp
import numpy as np
from jax import lax
from jax.experimental import pallas as pl
from jax.experimental.pallas import tpu as pltpu
from jax.sharding import Mesh
from jax.sharding import PartitionSpec as P

HEAD_DIM = 128
PAIR = 2 * HEAD_DIM
BEACONS = 4
STRETCH = 512
FEAT = 2048
PAIRS = FEAT // PAIR
LANES = 128
HALF = 256
BLOCK = 64
SCALE = HEAD_DIM ** (-0.5)
LOG_SCALE = SCALE * math.log2(math.e)
HIDDEN = -1e30
F32 = jnp.float32
BF16 = jnp.bfloat16

NAMES = ("x_lo", "z", "core", "y", "x_hi")
SIZES = (2, 4, 2, 4, 2)

X0, X1, Y0, Y1, Z0, Z1 = 1, 2, 4, 8, 16, 32
STEPS = ((Z1, Z0, X1, Y1, X0, Y0), (Y1, X0, Y0, Z1, Z0, X1))


def gray(position):
    return position ^ (position >> 1)


def slot_of(label, core):
    x, y, z = (gray((label >> shift) & 3) for shift in (0, 2, 4))
    return ((((x & 1) * 4 + z) * 2 + core) * 4 + y) * 2 + (x >> 1)


def exchange(value, step):
    pairs = []
    for label in range(64):
        for core in range(2):
            partner = label ^ STEPS[core][step]
            pairs.append((slot_of(label, core), slot_of(partner, core)))
    return lax.ppermute(value, NAMES, sorted(pairs))


def swap(value):
    return lax.ppermute(value, "core", [(0, 1), (1, 0)])


def beside(values, token, work):
    values, token = lax.optimization_barrier((values, token))
    return lax.optimization_barrier(work(values, token))


def joined(kept, got, axis=0):
    return lax.optimization_barrier(jnp.concatenate([kept, got], axis=axis))


def added(first, *more):
    total = first.astype(F32)
    for term in more:
        total = total + term.astype(F32)
    return total.astype(BF16)


def mask_kernel(assign_ref, prefix_ref, bias_ref):
    x_lo, z, core, y, x_hi = (lax.axis_index(name) for name in NAMES)
    mine = gray(x_hi * 2 + x_lo) | (gray(y) << 2) | (gray(z) << 4)
    own = slot_of(mine, core)
    numbers = lax.broadcasted_iota(jnp.int32, (1, LANES), 1)
    assign, prefix = assign_ref[...], prefix_ref[...]

    def pick(values, index):
        return jnp.sum(jnp.where(numbers == index, values, 0).astype(F32), axis=1, keepdims=True)

    stretch = pick(assign, own).astype(jnp.int32)
    lowest = stretch - pick(prefix, stretch).astype(jnp.int32)
    seen = jnp.where((assign >= lowest) & (assign < stretch), 1.0, 0.0)
    place = lax.broadcasted_iota(jnp.int32, (HALF, LANES), 0) >> 2
    labels = []
    for steps in STEPS:
        label = jnp.full((HALF, LANES), mine, jnp.int32)
        for step, bit in enumerate(steps):
            label = label ^ (((place >> step) & 1) * bit)
        labels.append(label)
    for half in range(2):
        label = jnp.where(core == half, labels[0], labels[1])
        slots = slot_of(label, core if half == 0 else 1 - core)
        found = jnp.sum(jnp.where(slots == numbers, seen, 0.0), axis=1, keepdims=True)
        rows = slice(half * HALF, (half + 1) * HALF)
        bias_ref[rows] = jnp.broadcast_to(jnp.where(found > 0.5, 0.0, HIDDEN), (HALF, LANES))


def far_bias(assign, prefix):
    line = pl.BlockSpec((1, LANES), lambda: (0, 0))
    return pl.pallas_call(
        mask_kernel,
        in_specs=[line, line],
        out_specs=pl.BlockSpec((2 * HALF, LANES), lambda: (0, 0)),
        out_shape=jax.ShapeDtypeStruct((2 * HALF, LANES), F32),
        name="far_mask",
    )(assign.reshape(1, LANES), prefix.reshape(1, LANES))


def spread(rows):
    twice = jnp.concatenate([rows.astype(F32)] * 2, axis=0)
    row = lax.broadcasted_iota(jnp.int32, twice.shape, 0)
    column = lax.broadcasted_iota(jnp.int32, twice.shape, 1)
    kept = jnp.where((row < BEACONS) == (column < HEAD_DIM), twice, 0.0)
    rest = jnp.zeros((LANES - 2 * BEACONS, rows.shape[1]), F32)
    return jnp.concatenate([kept, rest], axis=0).astype(BF16)


def padded(rows):
    rest = jnp.zeros((12, rows.shape[1]), F32)
    return jnp.concatenate([rows.astype(F32), rest], axis=0).astype(BF16)


def nt(a, b):
    return lax.dot_general(a, b, (((1,), (1,)), ((), ())), preferred_element_type=F32)


def nn(a, b):
    return lax.dot_general(a, b, (((1,), (0,)), ((), ())), preferred_element_type=F32)


def tn(a, b):
    return lax.dot_general(a, b, (((0,), (0,)), ((), ())), preferred_element_type=F32)


def top_of(scores):
    return jnp.max(scores, axis=0, keepdims=True)


def sum_of(values):
    return jnp.sum(values, axis=0, keepdims=True)


def causal(scores):
    rows = lax.broadcasted_iota(jnp.int32, scores.shape, 0)
    columns = lax.broadcasted_iota(jnp.int32, scores.shape, 1)
    return jnp.where(rows <= columns, scores, HIDDEN)


def own_mask(scores):
    rows = lax.broadcasted_iota(jnp.int32, scores.shape, 0)
    columns = lax.broadcasted_iota(jnp.int32, scores.shape, 1)
    return jnp.where((rows <= (columns & 3)) & (rows < BEACONS), scores, HIDDEN)


def power(scores, top):
    return jnp.exp2((scores - top) * LOG_SCALE)


def stats_of(parts):
    top = top_of(parts[0][0])
    for scores, _ in parts[1:]:
        top = jnp.maximum(top, top_of(scores))
    total = inner = None
    for scores, dprobs in parts:
        weights = power(scores, top)
        part, part_inner = sum_of(weights), sum_of(weights * dprobs)
        total = part if total is None else total + part
        inner = part_inner if inner is None else inner + part_inner
    return top, total, inner


def head(index):
    return slice(index * HEAD_DIM, (index + 1) * HEAD_DIM)


def raw_parts(q, k, v, g):
    low, high = slice(0, HALF), slice(HALF, 2 * HALF)
    s00 = causal(nt(k[low], q[low]))
    s01 = nt(k[low], q[high])
    s11 = causal(nt(k[high], q[high]))
    d00 = nt(v[low], g[low])
    d01 = nt(v[low], g[high])
    d11 = nt(v[high], g[high])
    return (s00, d00), (s01, d01), (s11, d11)


def stats_kernel(q_ref, k_ref, v_ref, g_ref, bq_ref, bk_ref, bv_ref, bg_ref, *refs):
    st_ref = refs[-1]
    qb, gb = spread(bq_ref[...]), spread(bg_ref[...])

    def products(index):
        if index < 0:
            raw = nt(k_ref[...], qb), nt(v_ref[...], gb)
            return raw, (own_mask(nt(padded(bk_ref[...]), qb)), nt(padded(bv_ref[...]), gb))
        columns = head(index)
        return raw_parts(
            q_ref[:, columns], k_ref[:, columns], v_ref[:, columns], g_ref[:, columns]
        )

    def store(index, *parts):
        if index < 0:
            found = ((STRETCH, LANES, stats_of(parts)),)
        else:
            p00, p01, p11 = parts
            found = ((0, HALF, stats_of([p00])), (HALF, HALF, stats_of([p01, p11])))
        for place, width, stats in found:
            for row, entry in enumerate(stats):
                row += 3 * max(index, 0)
                st_ref[row : row + 1, place : place + width] = entry

    pipelined([(-1,), (0,), (1,)], products, store)


def units_of(q_ref):
    return [(pair, index) for pair in range(q_ref.shape[1] // PAIR) for index in (-1, 0, 1)]


def columns_of(pair, index):
    if index < 0:
        return slice(pair * PAIR, (pair + 1) * PAIR)
    return head(2 * pair + index)


def block_columns(pair, index, value):
    start = 2 * pair * PAIR + (PAIR if value else 0)
    if index < 0:
        return slice(start, start + PAIR)
    return slice(start + index * HEAD_DIM, start + (index + 1) * HEAD_DIM)


def lanes_of(index):
    return slice(STRETCH, STAT_LANES) if index < 0 else slice(0, STRETCH)


def read_stats(ref, pair, index):
    base = 3 * max(index, 0)
    return tuple(ref[pair, base + row : base + row + 1, lanes_of(index)] for row in range(3))


def write_stats(ref, pair, index, stats):
    base = 3 * max(index, 0)
    for row, entry in enumerate(stats):
        ref[pair, base + row : base + row + 1, lanes_of(index)] = entry


def final_of(stats):
    top, total, inner = stats
    scaled = 1.0 / total
    return top, scaled, inner * scaled


def spread_pairs(*refs):
    pairs = refs[0].shape[1] // PAIR
    return [
        [spread(ref[:, pair * PAIR : (pair + 1) * PAIR]) for ref in refs] for pair in range(pairs)
    ]


def rows_of(refs, columns):
    return jnp.concatenate([ref[:, columns] for ref in refs], axis=0)


def pipelined(units, first, second):
    ready = first(*units[0])
    for place, unit in enumerate(units):
        now = ready
        if place + 1 < len(units):
            ready = first(*units[place + 1])
        second(*unit, *now)


def weighed(scores, dprobs, before, pair, index):
    known = [read_stats(ref, pair, index) for ref in before]
    top = top_of(scores)
    for stats in known:
        top = jnp.maximum(top, stats[0])
    weights = power(scores, top)
    total, inner = sum_of(weights), sum_of(weights * dprobs)
    for stats in known:
        factor = power(stats[0], top)
        total, inner = total + stats[1] * factor, inner + stats[2] * factor
    return weights, (top, total, inner)


def weigh_kernel(places, priors, *refs):
    q_ref, g_ref, bq_ref, bg_ref, bias_ref = refs[:5]
    blocks, before = refs[5 : 5 + len(places)], refs[5 + len(places) : 5 + len(places) + priors]
    w_ref, wb_ref, dp_ref, dpb_ref, out_ref = refs[-5:]
    bias = jnp.concatenate([bias_ref[place * BLOCK : (place + 1) * BLOCK] for place in places], 0)
    wide = jnp.concatenate([bias] * 4, axis=1)
    spreads = spread_pairs(bq_ref, bg_ref)

    def products(pair, index):
        columns = columns_of(pair, index)
        if index < 0:
            (q, g), hidden = spreads[pair], bias
        else:
            q, g, hidden = q_ref[:, columns], g_ref[:, columns], wide
        key = rows_of(blocks, block_columns(pair, index, False))
        value = rows_of(blocks, block_columns(pair, index, True))
        return nt(key, q) + hidden, nt(value, g)

    def weigh(pair, index, scores, dprobs):
        kept = dprobs.astype(BF16)
        weights, stats = weighed(scores, kept.astype(F32), before, pair, index)
        write_stats(out_ref, pair, index, stats)
        if index < 0:
            wb_ref[pair], dpb_ref[pair] = weights.astype(BF16), kept
        else:
            w_ref[2 * pair + index], dp_ref[2 * pair + index] = weights.astype(BF16), kept

    pipelined(units_of(q_ref), products, weigh)


def diagonal_kernel(places, priors, *refs):
    q_ref, g_ref, bq_ref, bg_ref, bias_ref = refs[:5]
    blocks, before = refs[5:7], refs[7 : 7 + priors]
    d_refs, ds_ref, dsb_ref, out_ref = refs[-5:-3], refs[-3], refs[-2], refs[-1]
    bias = jnp.concatenate([bias_ref[place * BLOCK : (place + 1) * BLOCK] for place in places], 0)
    wide = jnp.concatenate([bias] * 4, axis=1)
    spreads = spread_pairs(bq_ref, bg_ref)
    beacon = {}

    def products(pair, index):
        columns = columns_of(pair, index)
        if index < 0:
            (q, g), hidden = spreads[pair], bias
        else:
            q, g, hidden = q_ref[:, columns], g_ref[:, columns], wide
        key = rows_of(blocks, block_columns(pair, index, False))
        value = rows_of(blocks, block_columns(pair, index, True))
        return nt(key, q) + hidden, nt(value, g)

    def finish(pair, index, scores, dprobs):
        weights, stats = weighed(scores, dprobs, before, pair, index)
        write_stats(out_ref, pair, index, stats)
        _, scaled, inner = final_of(stats)
        probs = weights * scaled
        dscores = (probs * (dprobs - inner)).astype(BF16)
        store_terms(
            pair, index, probs.astype(BF16), dscores, beacon, spreads, q_ref, g_ref,
            d_refs, ds_ref, dsb_ref,
        )

    pipelined(units_of(q_ref), products, finish)


def store_terms(
    pair, index, probs, dscores, beacon, spreads, q_ref, g_ref, d_refs, ds_ref, dsb_ref
):
    if index < 0:
        qb, gb = spreads[pair]
        beacon[pair] = nn(dscores, qb), nn(probs, gb)
        dsb_ref[pair] = dscores
        return
    columns = columns_of(pair, index)
    dkey, dvalue = beacon[pair]
    ds_ref[2 * pair + index] = dscores
    head_key = ((nn(dscores, q_ref[:, columns]) + dkey[:, head(index)]) * SCALE).astype(BF16)
    head_value = (nn(probs, g_ref[:, columns]) + dvalue[:, head(index)]).astype(BF16)
    rows = head_key.shape[0] // len(d_refs)
    for place, d_ref in enumerate(d_refs):
        some = slice(place * rows, (place + 1) * rows)
        d_ref[:, block_columns(pair, index, False)] = head_key[some]
        d_ref[:, block_columns(pair, index, True)] = head_value[some]


def terms_kernel(counts, *refs):
    q_ref, g_ref, bq_ref, bg_ref, final_ref = refs[:5]
    calls = refs[5 : 5 + 5 * len(counts)]
    d_ref, ds_ref, dsb_ref = refs[-3:]
    spreads = spread_pairs(bq_ref, bg_ref)
    beacon = {}

    def products(pair, index):
        return ()

    def finish(pair, index):
        top, scaled, inner = final_of(read_stats(final_ref, pair, index))
        parts, dprobs = [], []
        for place in range(len(counts)):
            w_ref, wb_ref, dp_ref, dpb_ref, st_ref = calls[5 * place : 5 * place + 5]
            weights = wb_ref[pair] if index < 0 else w_ref[2 * pair + index]
            kept = dpb_ref[pair] if index < 0 else dp_ref[2 * pair + index]
            factor = power(read_stats(st_ref, pair, index)[0], top) * scaled
            parts.append(weights.astype(F32) * factor)
            dprobs.append(kept.astype(F32))
        probs, dprobs = jnp.concatenate(parts, axis=0), jnp.concatenate(dprobs, axis=0)
        dscores = (probs * (dprobs - inner)).astype(BF16)
        probs = probs.astype(BF16)
        store_terms(
            pair, index, probs, dscores, beacon, spreads, q_ref, g_ref, (d_ref,), ds_ref, dsb_ref
        )

    pipelined(units_of(q_ref), products, finish)


def split_grad(weights, dprobs, stats):
    _, scaled, inner = stats
    probs = weights * scaled
    return probs.astype(BF16), (probs * (dprobs - inner)).astype(BF16)


def grads(scores, dprobs, stats):
    return split_grad(power(scores, stats[0]), dprobs, stats)


def raw_kernel(*refs):
    q_ref, k_ref, v_ref, g_ref, bq_ref, bk_ref, bv_ref, bg_ref, st_ref = refs[:9]
    far = rows_of(refs[9:17], slice(0, PAIR))
    far_ds = refs[17:20]
    far_dsb = jnp.concatenate([ref[...] for ref in refs[20:23]], axis=0)
    dq_ref, dk_ref, dv_ref, dbq_ref, own_k_ref, own_v_ref = refs[-6:]
    qb, gb = spread(bq_ref[...]), spread(bg_ref[...])
    key, value = k_ref[...], v_ref[...]
    stats = final_of(tuple(st_ref[row : row + 1, STRETCH:] for row in range(3)))
    probs, dscores = grads(nt(key, qb), nt(value, gb), stats)
    dkey, dvalue = nn(dscores, qb), nn(probs, gb)
    dqb = tn(dscores, key) + tn(far_dsb, far)
    dqb = dqb[: 2 * BEACONS]
    own_key = padded(bk_ref[...])
    probs, dscores = grads(own_mask(nt(own_key, qb)), nt(padded(bv_ref[...]), gb), stats)
    own_k_ref[...] = nn(dscores, qb)[: 2 * BEACONS] * SCALE
    own_v_ref[...] = nn(probs, gb)[: 2 * BEACONS]
    dqb = (dqb + tn(dscores, own_key)[: 2 * BEACONS]) * SCALE
    dbq_ref[:, head(0)] = dqb[:BEACONS, head(0)].astype(BF16)
    dbq_ref[:, head(1)] = dqb[BEACONS:, head(1)].astype(BF16)
    low, high = slice(0, HALF), slice(HALF, 2 * HALF)

    def products(index):
        columns = head(index)
        return raw_parts(q_ref[:, columns], key[:, columns], value[:, columns], g_ref[:, columns])

    def finish(index, p00, p01, p11):
        columns = head(index)
        q, k, g = q_ref[:, columns], key[:, columns], g_ref[:, columns]
        stats = tuple(st_ref[3 * index + row : 3 * index + row + 1, :STRETCH] for row in range(3))
        stats = final_of(stats)
        first = tuple(entry[:, low] for entry in stats)
        second = tuple(entry[:, high] for entry in stats)
        probs00, ds00 = grads(*p00, first)
        probs01, ds01 = grads(*p01, second)
        probs11, ds11 = grads(*p11, second)
        dk_ref[low, columns] = (
            (nn(ds00, q[low]) + nn(ds01, q[high]) + dkey[low, columns]) * SCALE
        ).astype(BF16)
        dk_ref[high, columns] = ((nn(ds11, q[high]) + dkey[high, columns]) * SCALE).astype(BF16)
        dv_ref[low, columns] = (
            nn(probs00, g[low]) + nn(probs01, g[high]) + dvalue[low, columns]
        ).astype(BF16)
        dv_ref[high, columns] = (nn(probs11, g[high]) + dvalue[high, columns]).astype(BF16)
        ds_far = jnp.concatenate([ref[index] for ref in far_ds], axis=0)
        dq_far = tn(far[:, columns], ds_far)
        dq_low = dq_far[:, low] + tn(k[low], ds00)
        dq_high = dq_far[:, high] + tn(k[low], ds01) + tn(k[high], ds11)
        dq_ref[low, columns] = (dq_low.T * SCALE).astype(BF16)
        dq_ref[high, columns] = (dq_high.T * SCALE).astype(BF16)

    pipelined([(0,), (1,)], products, finish)


def three(rows, start=0, pairs=1):
    return pl.BlockSpec((None, rows, PAIR * pairs), lambda step: (0, 0, start + step))


def two(rows, start=0, pairs=1):
    return pl.BlockSpec((rows, PAIR * pairs), lambda step: (0, start + step))


def paired(rows, columns, start=0, pairs=None):
    return pl.BlockSpec((pairs, rows, columns), lambda step: (start + step, 0, 0))


def shape(dims, dtype):
    return jax.ShapeDtypeStruct(dims, dtype)


def params(megabytes):
    return pltpu.CompilerParams(
        dimension_semantics=("arbitrary",), vmem_limit_bytes=megabytes * 1024 * 1024
    )


def cost(flops, moved):
    return pl.CostEstimate(flops=flops, bytes_accessed=moved, transcendentals=0)


STAT_LANES = STRETCH + LANES


def pieces(kernel, start, count, inputs, in_specs, out_specs, out_shape, before, name, flops, megabytes):
    before = tuple(before)
    aliases = {len(inputs) + place: place for place in range(len(before))}
    return pl.pallas_call(
        kernel,
        grid=(count,),
        in_specs=in_specs + [pl.BlockSpec(memory_space=pl.ANY)] * len(before),
        out_specs=out_specs,
        out_shape=out_shape,
        input_output_aliases=aliases,
        compiler_params=params(megabytes),
        cost_estimate=cost(flops, 2**10),
        name=name,
    )(*inputs, *before)


def raw_stats(start, count, inputs, before):
    raw = three(STRETCH, start)
    return pieces(
        stats_kernel,
        start, count, inputs,
        [raw] * 4 + [three(BEACONS, start)] * 4,
        [paired(8, STAT_LANES, start)],
        [shape((PAIRS, 8, STAT_LANES), F32)],
        before, f"raw_stats_{start}", 10**6, 56,
    )


def raw_grads(start, count, inputs, before):
    raw = three(STRETCH, start)
    rows = (2 * BLOCK, 3 * BLOCK, 3 * BLOCK)
    return pieces(
        raw_kernel,
        start, count, inputs,
        [raw] * 4
        + [three(BEACONS, start)] * 4
        + [paired(8, STAT_LANES, start)]
        + [pl.BlockSpec((BLOCK, 2 * PAIR), lambda step: (0, start + step))] * 8
        + [paired(count_rows, STRETCH, start, 2) for count_rows in rows]
        + [paired(count_rows, LANES, start) for count_rows in rows],
        [raw] * 3 + [three(BEACONS, start)] + [two(8, start)] * 2,
        [shape((1, STRETCH, FEAT), BF16)] * 3
        + [shape((1, BEACONS, FEAT), BF16)]
        + [shape((8, FEAT), F32)] * 2,
        before, f"raw_grads_{start}", 10**6, 16,
    )


STEP_PAIRS = 2


def block_spec(rows=BLOCK):
    return pl.BlockSpec((rows, 2 * PAIR * STEP_PAIRS), lambda step: (0, step))


def some_rows(rows, columns, per_pair, place=0):
    return pl.BlockSpec((per_pair * STEP_PAIRS, rows, columns), lambda step: (step, place, 0))


def far_call(kernel, name, inputs, in_specs, out_specs, out_shape, flops):
    shared = [three(STRETCH, 0, STEP_PAIRS)] * 2 + [three(BEACONS, 0, STEP_PAIRS)] * 2
    return pl.pallas_call(
        kernel,
        grid=(PAIRS // STEP_PAIRS,),
        in_specs=shared + in_specs,
        out_specs=out_specs,
        out_shape=out_shape,
        compiler_params=params(12),
        cost_estimate=cost(flops, 2**10),
        name=name,
    )(*inputs)


def stat_spec():
    return paired(8, STAT_LANES, 0, STEP_PAIRS)


def weigh(places, queries, bias, blocks, before):
    rows = BLOCK * len(places)
    return far_call(
        lambda *refs: weigh_kernel(places, len(before), *refs),
        "far_weights_" + "_".join(map(str, places)),
        (*queries, bias, *blocks, *before),
        [pl.BlockSpec((2 * HALF, LANES), lambda step: (0, 0))]
        + [block_spec()] * len(places)
        + [stat_spec()] * len(before),
        [some_rows(rows, STRETCH, 2), some_rows(rows, LANES, 1)] * 2 + [stat_spec()],
        [shape((2 * PAIRS, rows, STRETCH), BF16), shape((PAIRS, rows, LANES), BF16)] * 2
        + [shape((PAIRS, 8, STAT_LANES), F32)],
        10**6,
    )


def terms(name, queries, final, calls):
    counts = tuple(count for _, count, _ in calls)
    rows = BLOCK * sum(counts)
    call_specs, call_inputs = [], []
    for outputs, count, place in calls:
        call_specs += [
            *[
                some_rows(BLOCK * count, STRETCH, 2, place),
                some_rows(BLOCK * count, LANES, 1, place),
            ]
            * 2,
            stat_spec(),
        ]
        call_inputs += list(outputs)
    return far_call(
        lambda *refs: terms_kernel(counts, *refs),
        name,
        (*queries, final, *call_inputs),
        [stat_spec()] + call_specs,
        [block_spec(rows), some_rows(rows, STRETCH, 2), some_rows(rows, LANES, 1)],
        [
            shape((rows, 2 * FEAT), BF16),
            shape((2 * PAIRS, rows, STRETCH), BF16),
            shape((PAIRS, rows, LANES), BF16),
        ],
        10**6,
    )


def diagonal_terms(queries, bias, blocks, before):
    rows = 2 * BLOCK
    return far_call(
        lambda *refs: diagonal_kernel((3, 7), len(before), *refs),
        "far_diagonal",
        (*queries, bias, *blocks, *before),
        [pl.BlockSpec((2 * HALF, LANES), lambda step: (0, 0))]
        + [block_spec()] * 2
        + [stat_spec()] * len(before),
        [block_spec()] * 2 + [some_rows(rows, STRETCH, 2), some_rows(rows, LANES, 1), stat_spec()],
        [shape((BLOCK, 2 * FEAT), BF16)] * 2
        + [
            shape((2 * PAIRS, rows, STRETCH), BF16),
            shape((PAIRS, rows, LANES), BF16),
            shape((PAIRS, 8, STAT_LANES), F32),
        ],
        10**6,
    )


def woven(both):
    parts = both.reshape(both.shape[0], 2, PAIRS, PAIR)
    return lax.optimization_barrier(parts.transpose(0, 2, 1, 3).reshape(both.shape))


def unwoven(both):
    parts = both.reshape(BEACONS, PAIRS, 2, PAIR)
    return parts[:, :, 0].reshape(BEACONS, FEAT), parts[:, :, 1].reshape(BEACONS, FEAT)


def on_device(
    raw_q, raw_k, raw_v, raw_grad, beacon_q, beacon_k, beacon_v, beacon_grad, assign, prefix
):
    raw = (raw_q, raw_k, raw_v, raw_grad)
    rest = (beacon_k, beacon_v, beacon_grad)

    def raw_stats_of(place, count, token, stats):
        return raw_stats(place, count, (*raw, token, *rest), stats)

    def queries(token):
        return raw_q, raw_grad, token, beacon_grad

    own0 = lax.optimization_barrier(jnp.concatenate([beacon_k[0], beacon_v[0]], axis=1))
    (got, bias) = beside(
        own0, assign, lambda value, token: (exchange(value, 0), far_bias(token, prefix))
    )
    own0 = woven(joined(own0, got))
    stats = ()
    for step, place, count in ((1, 0, 1), (2, 1, 1), (3, 2, 3)):
        got, stats = beside(
            own0,
            (beacon_q, stats),
            lambda value, token, step=step, place=place, count=count: (
                exchange(value, step), raw_stats_of(place, count, *token)
            ),
        )
        own0 = joined(own0, got)

    def stage_one(value, token):
        got = exchange(value, 4), exchange(value, 5), swap(value)
        stats = raw_stats_of(5, 3, *token)
        late, token, stats = lax.optimization_barrier((got[2], token[0], stats))
        return got, stats, weigh((0, 4), queries(token), bias, (value, late), ())

    (own_u, own_v, other0), stats, first = beside(own0, (beacon_q, stats), stage_one)

    def stage_two(values, token):
        own_u, own_v = values
        got = exchange(own_v[:, :FEAT], 4), exchange(own_u[:, FEAT:], 5)
        others = swap(own_u), swap(own_v)
        blocks = (own_u, own_v, *others)
        return got, others, weigh((1, 2, 5, 6), queries(token), bias, blocks, first[4:])

    (got_low, got_high), (other_u, other_v), second = beside((own_u, own_v), beacon_q, stage_two)
    own_uv = joined(got_low, got_high, axis=1)
    other_uv = swap(own_uv)
    d_own, d_other, ds_uv, dsb_uv, final = diagonal_terms(
        queries(beacon_q), bias, (own_uv, other_uv), (second[4], *stats)
    )
    got, others = beside(
        d_other,
        beacon_q,
        lambda value, token: (
            swap(value),
            terms(
                "other_rest", queries(token), final,
                [(first, 1, 1), (second, 2, 1)],
            ),
        ),
    )
    diagonal = added(d_own, got)

    def back_two(values, token):
        value, rest = values
        got = exchange(value[:, :FEAT], 4), exchange(value[:, FEAT:], 5)
        return got, swap(rest), terms(
            "own_rest", queries(token), final,
            [(first, 1, 0), (second, 2, 0)],
        )

    (got_low, got_high), got, owns = beside((diagonal, others[0]), beacon_q, back_two)
    blocks = [slice(place * BLOCK, (place + 1) * BLOCK) for place in range(3)]
    sums = [(owns[0][rows], got[rows]) for rows in blocks]
    none = jnp.zeros((BLOCK, FEAT), BF16)
    total = added(*sums[0])
    total_u = added(*sums[1], jnp.concatenate([none, got_high], axis=1))
    total_v = added(*sums[2], jnp.concatenate([got_low, none], axis=1))
    known = (
        final, own_uv, other_uv, other0, other_u, other_v, own0, own_u, own_v,
        ds_uv, others[1], owns[1], dsb_uv, others[2], owns[2],
    )

    def raw_grads_of(place, count, token, outs):
        return raw_grads(place, count, (*raw, token, *rest, *known), outs)

    (got_u, got_v), outs = beside(
        (total_u, total_v),
        beacon_q,
        lambda values, token: (
            (exchange(values[0], 4), exchange(values[1], 5)), raw_grads_of(0, 3, token, ())
        ),
    )
    total = added(total, got_u, got_v)
    for step, place, count in ((3, 3, 2), (2, 5, 1), (1, 6, 1), (0, 7, 1)):
        half = total.shape[0] // 2
        got, outs = beside(
            total[half:],
            (beacon_q, outs),
            lambda value, token, step=step, place=place, count=count: (
                exchange(value, step), raw_grads_of(place, count, *token)
            ),
        )
        kept = total[:half]
        if step:
            total = added(kept, got)
    raw_dq, raw_dk, raw_dv, beacon_dq, own_dk, own_dv = outs
    total_k, total_v = unwoven(kept.astype(F32) + got.astype(F32))
    beacon_dk = (own_dk[:BEACONS] + total_k).astype(BF16)[None]
    beacon_dv = (own_dv[:BEACONS] + total_v).astype(BF16)[None]
    return (raw_dq, raw_dk, raw_dv, beacon_dq, beacon_dk, beacon_dv)


def solution(mesh):
    named = Mesh(mesh.devices.reshape(SIZES), NAMES)
    placed = P(NAMES, None, None)
    return jax.shard_map(
        on_device,
        mesh=named,
        in_specs=(placed,) * 8 + (P(), P()),
        out_specs=(placed,) * 6,
        check_vma=False,
    )
```
